512 devices in a mesh: dp: 8 (over y, core), ctx: 32 (over z, x_hi), tp: 2 (over x_lo).
Axes of the slice: x: 4 (x_hi: 2, x_lo: 2; x = x_hi * 2 + x_lo), y: 4, z: 16, core: 2. Of those that a mesh axis runs over, the one named last changes fastest.
Arguments:
- query_states: bfloat16 [8, 4096, 1024], P('dp', 'ctx', 'tp'), may hold values from -9 to 9
- key_states: bfloat16 [8, 4096, 1024], P('dp', 'ctx', 'tp'), may hold values from -9 to 9
- value_states: bfloat16 [8, 4096, 1024], P('dp', 'ctx', 'tp'), may hold values from -6 to 6
- out_weight: bfloat16 [2048, 1024], P('ctx', 'tp'), may hold values from -1.5 to 1.5
- grad_output: bfloat16 [8, 4096, 2048], P('dp', 'ctx', 'tp'), may hold values from -0.625 to 0.625
- segment_table: int32 [8, 3, 5], P('dp'), may hold values from 0 to 4095, as said below
Outputs:
- layer_output: bfloat16 [8, 4096, 2048], P('dp', 'ctx', 'tp')
- grad_queries: bfloat16 [8, 4096, 1024], P('dp', 'ctx', 'tp')
- grad_keys: bfloat16 [8, 4096, 1024], P('dp', 'ctx', 'tp')
- grad_values: bfloat16 [8, 4096, 1024], P('dp', 'ctx', 'tp')
- grad_weight: float32 [2048, 1024], P('ctx', 'tp')
The draws below stay inside these ranges and needn't reach their ends.
Inputs may be any that keep to these rules, and one draw needn't show every extreme that they name: `segment_table`: row 0 holds the starts, row 1 the lengths and row 2 the flags (1 for an image, 0 for text) of 5 segments that tile the document in order. Text and image segments alternate, beginning and ending with text; every text segment has one token or more, the last text segment exactly one, and every image segment exactly 1024.
All inputs are finite; a program needn't handle non-finite values.
Results may differ from the reference program's by a relative error of at most 0.027.
Values may be sent and summed in bfloat16 or wider, within the bound.
A program may use at most 64 MiB of HBM per device.

```python
import jax
import jax.numpy as jnp
from jax import lax

D = 2048
H = 16
HS = 64
TOK_DEV = 128
SEQ = 4096
DOCS = 8
HD = 1024
IMG = 1024
NIMG = 2
S = 5
N_CTX = 32
N_TP = 2


def drawn_field(field_key, spread):
    return spread * jax.random.truncated_normal(field_key, -6.0, 6.0, (DOCS, SEQ, HD), jnp.float32)


def draw_query_states(key, part):
    key = jax.random.fold_in(key, 3)
    field_all = drawn_field(key, 1.5)
    return field_all.astype(jnp.bfloat16)


def draw_key_states(key, part):
    key = jax.random.fold_in(key, 7)
    field_all = drawn_field(key, 1.5)
    return field_all.astype(jnp.bfloat16)


def draw_segment_table(key, part):
    key = jax.random.fold_in(key, 5)
    text_total = SEQ - NIMG * IMG
    head_text = text_total - 1

    def one_document(doc_key):
        picks = jax.random.permutation(doc_key, max(1, head_text - 1))[:NIMG - 1] + 1
        cut_points = jnp.sort(picks).astype(jnp.int32)
        edges = jnp.concatenate([jnp.zeros((1,), jnp.int32), cut_points, jnp.full((1,), head_text, jnp.int32)])
        text_lengths = jnp.concatenate([edges[1:] - edges[:-1], jnp.ones((1,), jnp.int32)])
        lengths = jnp.zeros((S,), jnp.int32).at[0::2].set(text_lengths).at[1::2].set(IMG)
        seg_starts = jnp.concatenate([jnp.zeros((1,), jnp.int32), jnp.cumsum(lengths)[:-1].astype(jnp.int32)])
        flags = (jnp.arange(S, dtype=jnp.int32) % 2).astype(jnp.int32)
        return jnp.stack([seg_starts, lengths, flags])
    return jax.vmap(one_document)(jax.random.split(key, DOCS))


def raised(values, rng, source, target, shards_of, factor):
    def block_of(dim):
        return (jnp.arange(values.shape[dim]) // (values.shape[dim] // shards_of)).reshape((-1,) + (1,) * (values.ndim - 1 - dim))

    near = jax.random.permutation(rng, shards_of)[block_of(target)]
    second = (block_of(target) + shards_of // 2) % shards_of
    return jnp.where((block_of(source) == near) | (block_of(source) == second), factor * values, values)


def block_levels(own_key, shape, shards, smallest, largest):
    factor_of = 1.0
    for axis_at, parts in shards:
        heights = jax.random.uniform(jax.random.fold_in(jax.random.fold_in(own_key, 6), axis_at), (parts,), jnp.float32, smallest / len(shards), largest / len(shards))
        factor_of = factor_of * jnp.repeat(jnp.exp(heights), shape[axis_at] // parts).reshape((-1,) + (1,) * (len(shape) - 1 - axis_at))
    return factor_of


def scatter_about(stream_key, dims, scale, bound, shards=(), held_as=jnp.bfloat16):
    loudness = block_levels(stream_key, dims, shards, -0.22, 0.18) if shards else 1.0
    values = jax.random.normal(stream_key, dims, jnp.float32) * scale * loudness
    return jnp.minimum(jnp.maximum(values, -bound), bound).astype(held_as)


def bell_draw_with(own_key, extent, width, limit, shards, heavy, held_as=jnp.bfloat16):
    drawn = width * jax.random.normal(own_key, extent, jnp.float32)
    if shards:
        drawn = drawn * block_levels(own_key, extent, shards, -0.22, 0.18)
    return jnp.clip(raised(drawn, jax.random.fold_in(own_key, 3), *heavy), -limit, limit).astype(held_as)


def setup_inputs(seed: int = 0) -> dict:
    seeds = jax.random.split(jax.random.key(seed), 7)
    return {
        "query_states": draw_query_states(jax.random.fold_in(seeds[6], 71), 0),
        "key_states": draw_key_states(jax.random.fold_in(seeds[6], 71), 0),
        "value_states": scatter_about(seeds[2], (DOCS, SEQ, HD), 1.0, 6.0, ((0, 8), (1, 32), (2, 2))),
        "out_weight": scatter_about(seeds[3], (D, HD), 0.25, 1.5, ((0, 32), (1, 2))),
        "grad_output": bell_draw_with(seeds[4], (DOCS, SEQ, D), 0.05, 0.625, ((0, 8), (1, 32), (2, 2)), (1, 2, 32, 2.75)),
        "segment_table": draw_segment_table(jax.random.fold_in(seeds[6], 71), 0),
    }


NEG_FILL = -1.0e30


def reach_of(seg_table, positions):
    seg_starts = seg_table[0]
    seg_ends = seg_table[0] + seg_table[1]
    is_image = seg_table[2] == 1
    inside = (positions[:, None] >= seg_starts[None, :]) & (positions[:, None] < seg_ends[None, :])
    image_hit = inside & is_image[None, :]
    image_last = jnp.sum(jnp.where(image_hit, seg_ends[None, :] - 1, 0), axis=1)
    return jnp.where(jnp.any(image_hit, axis=1), image_last, positions).astype(jnp.int32)


def head_forward(head_items, allowed, score_scale):
    query_rows, key_rows, value_rows = head_items
    scores = jnp.where(allowed, score_scale * jnp.dot(query_rows, key_rows.T, preferred_element_type=jnp.float32), NEG_FILL)
    row_top = jnp.max(scores, axis=1)
    exp_terms = jnp.where(allowed, jnp.exp(scores - row_top[:, None]), 0.0)
    log_total = row_top + jnp.log(jnp.sum(exp_terms, axis=1))
    probs = jnp.where(allowed, jnp.exp(scores - log_total[:, None]), 0.0)
    head_out = jnp.dot(probs.astype(jnp.bfloat16), value_rows, preferred_element_type=jnp.float32).astype(jnp.bfloat16)
    return head_out, log_total


def head_backward(head_items, allowed, score_scale):
    query_rows, key_rows, value_rows, head_out, log_total, grad_rows = head_items
    scores = jnp.where(allowed, score_scale * jnp.dot(query_rows, key_rows.T, preferred_element_type=jnp.float32), NEG_FILL)
    probs = jnp.where(allowed, jnp.exp(scores - log_total[:, None]), 0.0)
    probs_low = probs.astype(jnp.bfloat16)
    row_delta = jnp.sum(grad_rows.astype(jnp.float32) * head_out.astype(jnp.float32), axis=1)
    grad_probs = jnp.dot(grad_rows, value_rows.T, preferred_element_type=jnp.float32)
    grad_scores = (probs * (grad_probs - row_delta[:, None])).astype(jnp.bfloat16)
    grad_query = (score_scale * jnp.dot(grad_scores, key_rows, preferred_element_type=jnp.float32)).astype(jnp.bfloat16)
    grad_key = (score_scale * jnp.dot(grad_scores.T, query_rows, preferred_element_type=jnp.float32)).astype(jnp.bfloat16)
    grad_value = jnp.dot(probs_low.T, grad_rows, preferred_element_type=jnp.float32).astype(jnp.bfloat16)
    return grad_query, grad_key, grad_value


def by_heads(matrix):
    return matrix.reshape(SEQ, H, HS).transpose(1, 0, 2)


def by_tokens(stacked):
    return stacked.transpose(1, 0, 2).reshape(SEQ, H * HS)


def reference(query_states, key_states, value_states, out_weight, grad_output, segment_table):
    score_scale = HS ** -0.5
    width_tp = H * HS // N_TP
    positions = jnp.arange(SEQ, dtype=jnp.int32)

    def one_document(doc_items):
        query_doc, key_doc, value_doc, grad_doc, seg_table = doc_items
        reach = reach_of(seg_table, positions)
        allowed = positions[None, :] <= reach[:, None]
        head_outs, log_totals = lax.map(lambda head_items: head_forward(head_items, allowed, score_scale), (by_heads(query_doc), by_heads(key_doc), by_heads(value_doc)))
        attn = by_tokens(head_outs)
        out_total = jnp.zeros((SEQ, D), jnp.float32)
        for tp_index in range(N_TP):
            attn_half = attn[:, tp_index * width_tp:(tp_index + 1) * width_tp]
            weight_half = out_weight[:, tp_index * width_tp:(tp_index + 1) * width_tp]
            out_partial = jnp.dot(attn_half, weight_half.T, preferred_element_type=jnp.float32).astype(jnp.bfloat16)
            out_partial = lax.optimization_barrier(out_partial)
            out_total = out_total + out_partial.astype(jnp.float32)
        layer_doc = out_total.astype(jnp.bfloat16)
        grad_attn = jnp.dot(grad_doc, out_weight, preferred_element_type=jnp.float32).astype(jnp.bfloat16)
        grad_query, grad_key, grad_value = lax.map(lambda head_items: head_backward(head_items, allowed, score_scale), (by_heads(query_doc), by_heads(key_doc), by_heads(value_doc), head_outs, log_totals, by_heads(grad_attn)))
        grad_blocks = grad_doc.reshape(N_CTX, TOK_DEV, D).astype(jnp.float32)
        attn_blocks = attn.reshape(N_CTX, TOK_DEV, H * HS).astype(jnp.float32)
        weight_partial = jnp.einsum("ctd,cth->cdh", grad_blocks, attn_blocks, precision=lax.Precision.HIGHEST).astype(jnp.bfloat16)
        weight_partial = lax.optimization_barrier(weight_partial)
        weight_doc = jnp.sum(weight_partial.astype(jnp.float32), axis=0)
        return layer_doc, by_tokens(grad_query), by_tokens(grad_key), by_tokens(grad_value), weight_doc

    layer_output, grad_queries, grad_keys, grad_values, weight_docs = lax.map(one_document, (query_states, key_states, value_states, grad_output, segment_table))
    return (layer_output, grad_queries, grad_keys, grad_values, jnp.sum(weight_docs, axis=0))
```

```python
import functools

import jax
import jax.numpy as jnp
from jax import lax
from jax.experimental import pallas as pl
from jax.experimental.pallas import tpu as pltpu
from jax.sharding import PartitionSpec as P

MESH = pl.DeviceIdType.MESH
HS = 64
NEG_FILL = -1e30
TILE = 512
BF = jnp.bfloat16
F32 = jnp.float32
VMEM_LIMIT = 56 * 2**20


def swap_halves(first, second):
    low = lax.broadcasted_iota(jnp.int32, first.shape, 1) < HS
    first, second = first.astype(F32), second.astype(F32)
    return (
        jnp.where(low, first, pltpu.roll(second, HS, 1)).astype(BF),
        jnp.where(low, pltpu.roll(first, HS, 1), second).astype(BF),
    )


def remote(src, dst, send_sem, recv_sem, device):
    return pltpu.make_async_remote_copy(
        src_ref=src,
        dst_ref=dst,
        send_sem=send_sem,
        recv_sem=recv_sem,
        device_id=device,
        device_id_type=MESH,
    )


def places():
    ctx = lax.axis_index("ctx")
    dp = lax.axis_index("dp")
    tp = lax.axis_index("tp")
    return ctx, ctx // 4, ctx % 4, dp // 2, dp % 2, tp


def flip_x(member):
    return member + 1 - 2 * (member % 2)


def flip_z(member):
    return member + 2 - 4 * (member // 2)


def greet(devices):
    barrier = pltpu.get_barrier_semaphore()
    for device in devices:
        pl.semaphore_signal(barrier, inc=1, device_id=device, device_id_type=MESH)
    return lambda: pl.semaphore_wait(barrier, len(devices))


def gather_kernel(
    q_ref, k_ref, v_ref, w_ref, g_ref,
    qh_ref, kv_ref, gh_ref, wf_ref, gf_ref,
    kv_out, q_out, g_out,
    local_sem, kv_s, kv_r, q_s, q_r, w_s, w_r, gh_s, gh_r, m_s, m_r, y_s, y_r, one_s, one_r,
):
    ctx, spot, member, row, core, tp = places()
    peers = [{"ctx": ((spot + i) % 8) * 4 + member} for i in range(1, 8)]
    sources = [(spot + 8 - i) % 8 for i in range(1, 8)]
    x_dev = {"ctx": spot * 4 + flip_x(member)}
    z_dev = {"ctx": spot * 4 + flip_z(member)}
    y_devs = [{"dp": ((row + i) % 4) * 2 + core} for i in range(1, 4)]
    core_dev = {"dp": row * 2 + 1 - core}
    tp_dev = {"tp": 1 - tp}
    ready = greet(peers + [x_dev, z_dev] + y_devs + [core_dev, tp_dev])

    w_rows = pl.ds(pl.multiple_of(core * 32, 32), 32)
    w_cols = pl.ds(pl.multiple_of(row * 128, 128), 128)
    w_piece = w_ref.at[w_rows, w_cols]
    own_w = pltpu.make_async_copy(w_piece, wf_ref.at[spot, member, w_rows, w_cols], local_sem.at[0])
    own_g = pltpu.make_async_copy(g_ref, gf_ref.at[tp], local_sem.at[1])
    own_w.start()
    own_g.start()
    for pair in range(4):
        cols = slice(pair * 128, (pair + 1) * 128)
        even, odd = swap_halves(k_ref[:, cols], v_ref[:, cols])
        kv_out[2 * pair] = even
        kv_out[2 * pair + 1] = odd
        even, odd = swap_halves(q_ref[:64, cols], q_ref[64:, cols])
        q_out[2 * pair] = even
        q_out[2 * pair + 1] = odd
    own_kv = pltpu.make_async_copy(kv_out.at[spot], kv_ref.at[spot, member], local_sem.at[2])
    own_q = pltpu.make_async_copy(q_out.at[spot], qh_ref.at[spot], local_sem.at[3])
    own_kv.start()
    own_q.start()
    ready()

    sent = []

    def send(*copy_args):
        copy = remote(*copy_args)
        copy.start()
        sent.append(copy)

    def got(dst, recv_sem):
        remote(dst, dst, one_s.at[0], recv_sem, core_dev).wait_recv()

    for i in range(7):
        send(w_piece, wf_ref.at[spot, member, w_rows, w_cols], w_s.at[i], w_r.at[i], peers[i])
    send(g_ref, gf_ref.at[tp], one_s.at[0], one_r.at[0], tp_dev)
    for i in range(7):
        send(kv_out.at[(spot + i + 1) % 8], kv_ref.at[spot, member], kv_s.at[i], kv_r.at[i], peers[i])
    for i in range(7):
        send(q_out.at[(spot + i + 1) % 8], qh_ref.at[spot], q_s.at[i], q_r.at[i], peers[i])

    def w_slab(which):
        return wf_ref.at[:, which, w_rows, w_cols]

    def kv_slab(which):
        return kv_ref.at[:, which]

    own_w.wait()
    for i in range(7):
        got(wf_ref.at[sources[i], member, w_rows, w_cols], w_r.at[i])
    send(w_slab(member), w_slab(member), m_s.at[0], m_r.at[0], x_dev)
    send(w_slab(member), w_slab(member), m_s.at[1], m_r.at[1], z_dev)
    own_kv.wait()
    for i in range(7):
        got(kv_ref.at[sources[i], member], kv_r.at[i])
    send(kv_slab(member), kv_slab(member), m_s.at[3], m_r.at[3], x_dev)
    send(kv_slab(member), kv_slab(member), m_s.at[4], m_r.at[4], z_dev)
    got(w_slab(flip_x(member)), m_r.at[0])
    send(w_slab(flip_x(member)), w_slab(flip_x(member)), m_s.at[2], m_r.at[2], z_dev)
    got(w_slab(flip_z(member)), m_r.at[1])
    got(w_slab(flip_z(flip_x(member))), m_r.at[2])
    w_part = wf_ref.at[:, :, w_rows, w_cols]
    for i in range(3):
        send(w_part, w_part, y_s.at[i], y_r.at[i], y_devs[i])
    got(kv_slab(flip_x(member)), m_r.at[3])
    send(kv_slab(flip_x(member)), kv_slab(flip_x(member)), m_s.at[5], m_r.at[5], z_dev)
    for i in range(3):
        from_row = (row + 3 - i) % 4
        got(wf_ref.at[:, :, w_rows, pl.ds(pl.multiple_of(from_row * 128, 128), 128)], y_r.at[i])
    w_half = wf_ref.at[:, :, w_rows, :]
    send(w_half, w_half, one_s.at[1], one_r.at[1], core_dev)
    own_g.wait()
    got(gf_ref.at[1 - tp], one_r.at[0])
    got(wf_ref.at[:, :, pl.ds(pl.multiple_of(32 - core * 32, 32), 32), :], one_r.at[1])

    weight = wf_ref[...].reshape(2048, 512)
    grad_attn = jnp.dot(gf_ref[0], weight[:1024], preferred_element_type=F32)
    grad_attn += jnp.dot(gf_ref[1], weight[1024:], preferred_element_type=F32)
    grad_attn = grad_attn.astype(BF)
    for pair in range(4):
        cols = slice(pair * 128, (pair + 1) * 128)
        even, odd = swap_halves(grad_attn[:64, cols], grad_attn[64:, cols])
        g_out[2 * pair] = even
        g_out[2 * pair + 1] = odd
    own_gh = pltpu.make_async_copy(g_out.at[spot], gh_ref.at[spot], local_sem.at[4])
    own_gh.start()
    for i in range(7):
        send(g_out.at[(spot + i + 1) % 8], gh_ref.at[spot], gh_s.at[i], gh_r.at[i], peers[i])
    own_q.wait()
    own_gh.wait()
    for i in range(7):
        got(qh_ref.at[sources[i]], q_r.at[i])
    got(kv_slab(flip_z(member)), m_r.at[4])
    got(kv_slab(flip_z(flip_x(member))), m_r.at[5])
    for i in range(7):
        got(gh_ref.at[sources[i]], gh_r.at[i])
    for copy in sent:
        copy.wait_send()


def attention_kernel(seg_ref, q_ref, g_ref, kv_ref, ap_ref, dq_ref, dkv_ref, s_ref, dp_ref, p_ref, acc_ref):
    member = lax.axis_index("ctx") % 4
    low = lax.broadcasted_iota(jnp.int32, (64, 128), 1) < HS
    acc_ref[...] = jnp.zeros_like(acc_ref)

    def reach_of(position):
        reach = position
        for seg in range(5):
            start, length, flag = seg_ref[0, seg], seg_ref[1, seg], seg_ref[2, seg]
            inside = (position >= start) & (position < start + length) & (flag == 1)
            reach = jnp.where(inside, start + length - 1, reach)
        return reach

    def fold(tile, op):
        parts = [tile[:, c * 128:(c + 1) * 128] for c in range(TILE // 128)]
        while len(parts) > 1:
            parts = [op(parts[c], parts[c + 1]) for c in range(0, len(parts), 2)]
        return parts[0]

    def block(index, carry):
        begin = (4 * index + member) * 128
        qp = q_ref[index].astype(F32) * HS ** -0.5
        gp = g_ref[index].astype(F32)
        query = jnp.concatenate(
            [jnp.where(low, qp, 0.0), jnp.where(low, pltpu.roll(qp, HS, 1), 0.0)], axis=0
        )
        grad = jnp.concatenate(
            [jnp.where(low, 0.0, pltpu.roll(gp, HS, 1)), jnp.where(low, 0.0, gp)], axis=0
        )
        both = jnp.concatenate([query.astype(BF), grad.astype(BF)], axis=0)
        reach = reach_of(begin + lax.broadcasted_iota(jnp.int32, (128, 1), 0))
        tiles = reach_of(begin + 127) // TILE + 1

        def score(t, top):
            keys = pl.ds(pl.multiple_of(t * TILE, TILE), TILE)
            product = lax.dot_general(
                both, kv_ref[keys, :], (((1,), (1,)), ((), ())), preferred_element_type=F32
            )
            offset = t * TILE + lax.broadcasted_iota(jnp.int32, (128, TILE), 1)
            scores = jnp.where(offset <= reach, product[:128], NEG_FILL)
            s_ref[:, keys] = scores
            dp_ref[:, keys] = product[128:]
            return jnp.maximum(top, fold(scores, jnp.maximum))

        top = lax.fori_loop(0, tiles, score, jnp.full((128, 128), NEG_FILL, F32))
        top = jnp.max(top, axis=1, keepdims=True)

        def mix(t, carry):
            total, out = carry
            keys = pl.ds(pl.multiple_of(t * TILE, TILE), TILE)
            probs = jnp.exp(s_ref[:, keys] - top)
            probs_low = probs.astype(BF)
            p_ref[:, keys] = probs_low
            out = out + jnp.dot(probs_low, kv_ref[keys, :], preferred_element_type=F32)
            return total + fold(probs, jnp.add), out

        zeros = jnp.zeros((128, 128), F32)
        total, out = lax.fori_loop(0, tiles, mix, (zeros, zeros))
        inverse = 1.0 / jnp.sum(total, axis=1, keepdims=True)
        out = (out * inverse).astype(BF).astype(F32)
        delta = jnp.sum(grad * out, axis=1, keepdims=True)
        ap_ref[index] = jnp.where(low, pltpu.roll(out[:64], HS, 1), out[64:]).astype(BF)
        rows = jnp.concatenate([(query * inverse).astype(BF), (grad * inverse).astype(BF)], axis=0)

        def back(t, grad_query):
            keys = pl.ds(pl.multiple_of(t * TILE, TILE), TILE)
            probs_low = p_ref[:, keys]
            grad_scores = (probs_low.astype(F32) * (dp_ref[:, keys] - delta)).astype(BF)
            stacked = jnp.concatenate([grad_scores, probs_low], axis=0)
            acc_ref[keys, :] += lax.dot_general(
                stacked, rows, (((0,), (0,)), ((), ())), preferred_element_type=F32
            )
            return grad_query + jnp.dot(grad_scores, kv_ref[keys, :], preferred_element_type=F32)

        grad_query = lax.fori_loop(0, tiles, back, zeros) * (inverse * HS ** -0.5)
        dq_ref[index] = jnp.where(low, grad_query[:64], pltpu.roll(grad_query[64:], HS, 1)).astype(BF)
        return carry

    lax.fori_loop(0, 8, block, 0)
    dkv_ref[...] = acc_ref[...].astype(BF)


def return_kernel(
    ap_ref, dq_ref, dkv_ref, wf_ref, gf_ref,
    out_ref, gq_ref, gk_ref, gv_ref, gw_ref,
    a_in, dq_in, kv_in, z_in, z_sum, x_in, kv_sum, tp_out, tp_in,
    wp, core_in, core_sum, y_in, y_sum, m_in, m_sum, s_in, piece,
    local_sem, a_s, a_r, dq_s, dq_r, kv_s, kv_r, z_s, z_r, x_s, x_r,
    y_s, y_r, m_s, m_r, s_s, s_r, d_s, d_r, one_s, one_r,
):
    ctx, spot, member, row, core, tp = places()
    peers = [{"ctx": ((spot + i) % 8) * 4 + member} for i in range(1, 8)]
    sources = [(spot + 8 - i) % 8 for i in range(1, 8)]
    group = [{"ctx": spot * 4 + (member + i) % 4} for i in range(1, 4)]
    x_dev = {"ctx": spot * 4 + flip_x(member)}
    z_dev = {"ctx": spot * 4 + flip_z(member)}
    dp = row * 2 + core
    dp_devs = [{"dp": (dp + i) % 8} for i in range(1, 8)]
    y_devs = [{"dp": ((row + i) % 4) * 2 + core} for i in range(1, 4)]
    core_dev = {"dp": row * 2 + 1 - core}
    tp_dev = {"tp": 1 - tp}
    ready = greet(peers + group + dp_devs + [tp_dev])
    ready()

    sent = []

    def send(*copy_args):
        copy = remote(*copy_args)
        copy.start()
        sent.append(copy)

    def got(dst, recv_sem):
        remote(dst, dst, one_s.at[0], recv_sem, core_dev).wait_recv()

    z_bit, x_bit = member // 2, member % 2
    own_a = pltpu.make_async_copy(ap_ref.at[spot], a_in.at[spot], local_sem.at[0])
    own_dq = pltpu.make_async_copy(dq_ref.at[spot], dq_in.at[spot], local_sem.at[1])
    own_a.start()
    own_dq.start()
    for i in range(7):
        send(ap_ref.at[(spot + i + 1) % 8], a_in.at[spot], a_s.at[i], a_r.at[i], peers[i])
    for half in range(2):
        blocks = pl.ds(half * 4, 4)
        send(dkv_ref.at[blocks, pl.ds(2 - 2 * z_bit, 2)], z_in.at[blocks], z_s.at[half], z_r.at[half], z_dev)
    for i in range(7):
        send(dq_ref.at[(spot + i + 1) % 8], dq_in.at[spot], dq_s.at[i], dq_r.at[i], peers[i])

    own_a.wait()
    for i in range(7):
        got(a_in.at[sources[i]], a_r.at[i])
    tops, bottoms = [], []
    for pair in range(4):
        top, bottom = swap_halves(a_in[2 * pair], a_in[2 * pair + 1])
        tops.append(top)
        bottoms.append(bottom)
    attn = jnp.concatenate(
        [jnp.concatenate(tops, axis=1), jnp.concatenate(bottoms, axis=1)], axis=0
    )
    for half in range(2):
        part = lax.dot_general(
            gf_ref[half], attn, (((0,), (0,)), ((), ())), preferred_element_type=F32
        )
        wp[pl.ds(half * 4, 4)] = part.astype(BF).reshape(4, 4, 2, 32, 512)
    send(wp.at[:, :, 1 - core], core_in, one_s.at[1], one_r.at[1], core_dev)

    weight = wf_ref[...].reshape(2, 1024, 512)
    for half in range(2):
        part = lax.dot_general(
            attn, weight[half], (((1,), (1,)), ((), ())), preferred_element_type=F32
        )
        tp_out[half] = part.astype(BF)
    send(tp_out.at[1 - tp], tp_in, one_s.at[0], one_r.at[0], tp_dev)

    for half in range(2):
        blocks = pl.ds(half * 4, 4)
        got(z_in.at[blocks], z_r.at[half])
        z_sum[blocks] = (
            dkv_ref[blocks, pl.ds(2 * z_bit, 2)].astype(F32) + z_in[blocks].astype(F32)
        ).astype(BF)
        send(z_sum.at[blocks, 1 - x_bit], x_in.at[blocks], x_s.at[half], x_r.at[half], x_dev)

    got(core_in, one_r.at[1])
    core_sum[...] = (wp[:, :, core].astype(F32) + core_in[...].astype(F32)).astype(BF)
    for i in range(3):
        to_row = (row + i + 1) % 4
        cols = pl.ds(pl.multiple_of(to_row * 128, 128), 128)
        send(core_sum.at[:, :, :, cols], y_in.at[i], y_s.at[i], y_r.at[i], y_devs[i])

    for half in range(2):
        blocks = pl.ds(half * 4, 4)
        got(x_in.at[blocks], x_r.at[half])
        kv_sum[blocks] = (z_sum[blocks, x_bit].astype(F32) + x_in[blocks].astype(F32)).astype(BF)
    own_kv = pltpu.make_async_copy(kv_sum.at[spot], kv_in.at[spot], local_sem.at[2])
    own_kv.start()
    for i in range(7):
        send(kv_sum.at[(spot + i + 1) % 8], kv_in.at[spot], kv_s.at[i], kv_r.at[i], peers[i])

    got(tp_in, one_r.at[0])
    out_ref[...] = (tp_out[tp].astype(F32) + tp_in[...].astype(F32)).astype(BF)

    for i in range(3):
        got(y_in.at[i], y_r.at[i])
    cols = pl.ds(pl.multiple_of(row * 128, 128), 128)
    y_sum[...] = (
        (core_sum[:, :, :, cols].astype(F32) + y_in[0].astype(F32))
        + (y_in[1].astype(F32) + y_in[2].astype(F32))
    ).astype(BF)
    for i in range(3):
        send(y_sum.at[:, (member + i + 1) % 4], m_in.at[i], m_s.at[i], m_r.at[i], group[i])

    own_dq.wait()
    for i in range(7):
        got(dq_in.at[sources[i]], dq_r.at[i])
    for pair in range(4):
        cols = slice(pair * 128, (pair + 1) * 128)
        top, bottom = swap_halves(dq_in[2 * pair], dq_in[2 * pair + 1])
        gq_ref[:64, cols] = top
        gq_ref[64:, cols] = bottom

    for i in range(3):
        got(m_in.at[i], m_r.at[i])
    m_sum[...] = (
        (y_sum[:, member].astype(F32) + m_in[0].astype(F32))
        + (m_in[1].astype(F32) + m_in[2].astype(F32))
    ).astype(BF)
    for i in range(7):
        send(m_sum.at[(spot + i + 1) % 8], s_in.at[i], s_s.at[i], s_r.at[i], peers[i])

    own_kv.wait()
    for i in range(7):
        got(kv_in.at[sources[i]], kv_r.at[i])
    for pair in range(4):
        cols = slice(pair * 128, (pair + 1) * 128)
        keys, values = swap_halves(kv_in[2 * pair], kv_in[2 * pair + 1])
        gk_ref[:, cols] = keys
        gv_ref[:, cols] = values

    total = m_sum[spot].astype(F32)
    for i in range(7):
        got(s_in.at[i], s_r.at[i])
        total = total + s_in[i].astype(F32)
    piece[...] = total
    spot_w = gw_ref.at[
        pl.ds(pl.multiple_of(core * 32, 32), 32), pl.ds(pl.multiple_of(row * 128, 128), 128)
    ]
    own_w = pltpu.make_async_copy(piece, spot_w, local_sem.at[3])
    own_w.start()
    for i in range(7):
        send(piece, spot_w, d_s.at[i], d_r.at[i], dp_devs[i])
    own_w.wait()
    for i in range(7):
        source = (dp + 7 - i) % 8
        got(
            gw_ref.at[
                pl.ds(pl.multiple_of((source % 2) * 32, 32), 32),
                pl.ds(pl.multiple_of((source // 2) * 128, 128), 128),
            ],
            d_r.at[i],
        )
    for copy in sent:
        copy.wait_send()


def like(shape, dtype=BF):
    return jax.ShapeDtypeStruct(shape, dtype)


def dma(count):
    return pltpu.SemaphoreType.DMA((count,))


def body(query_states, key_states, value_states, out_weight, grad_output, segment_table):
    vmem = pl.BlockSpec(memory_space=pltpu.VMEM)
    smem = pl.BlockSpec(memory_space=pltpu.SMEM)
    scratch = lambda *shape: pltpu.VMEM(shape, BF)
    qh, kv, gh, wf, gf = pl.pallas_call(
        gather_kernel,
        out_shape=(
            like((8, 64, 128)),
            like((8, 4, 128, 128)),
            like((8, 64, 128)),
            like((8, 4, 64, 512)),
            like((2, 128, 1024)),
        ),
        in_specs=[vmem] * 5,
        out_specs=(vmem,) * 5,
        scratch_shapes=[
            scratch(8, 128, 128),
            scratch(8, 64, 128),
            scratch(8, 64, 128),
            dma(5),
            *[dma(7)] * 8,
            *[dma(6)] * 2,
            *[dma(3)] * 2,
            *[dma(2)] * 2,
        ],
        compiler_params=pltpu.CompilerParams(
            collective_id=0, has_side_effects=True, vmem_limit_bytes=VMEM_LIMIT
        ),
        name="gather_heads",
    )(query_states[0], key_states[0], value_states[0], out_weight, grad_output[0])
    ap, dq, dkv = pl.pallas_call(
        attention_kernel,
        out_shape=(like((8, 64, 128)), like((8, 64, 128)), like((4096, 128))),
        in_specs=[smem] + [vmem] * 3,
        out_specs=(vmem,) * 3,
        scratch_shapes=[
            pltpu.VMEM((128, 4096), F32),
            pltpu.VMEM((128, 4096), F32),
            pltpu.VMEM((128, 4096), BF),
            pltpu.VMEM((4096, 128), F32),
        ],
        compiler_params=pltpu.CompilerParams(vmem_limit_bytes=VMEM_LIMIT),
        name="attention",
    )(segment_table[0], qh, gh, kv.reshape(4096, 128))
    outs = pl.pallas_call(
        return_kernel,
        out_shape=(
            like((128, 1024)),
            like((128, 512)),
            like((128, 512)),
            like((128, 512)),
            like((64, 512), F32),
        ),
        in_specs=[vmem] * 5,
        out_specs=(vmem,) * 5,
        scratch_shapes=[
            scratch(8, 64, 128),
            scratch(8, 64, 128),
            scratch(8, 128, 128),
            scratch(8, 2, 128, 128),
            scratch(8, 2, 128, 128),
            scratch(8, 128, 128),
            scratch(8, 128, 128),
            scratch(2, 128, 1024),
            scratch(128, 1024),
            scratch(8, 4, 2, 32, 512),
            scratch(8, 4, 32, 512),
            scratch(8, 4, 32, 512),
            scratch(3, 8, 4, 32, 128),
            scratch(8, 4, 32, 128),
            scratch(3, 8, 32, 128),
            scratch(8, 32, 128),
            scratch(7, 32, 128),
            pltpu.VMEM((32, 128), F32),
            dma(4),
            *[dma(7)] * 6,
            *[dma(2)] * 4,
            *[dma(3)] * 4,
            *[dma(7)] * 4,
            *[dma(2)] * 2,
        ],
        compiler_params=pltpu.CompilerParams(
            collective_id=1, has_side_effects=True, vmem_limit_bytes=VMEM_LIMIT
        ),
        name="return_tokens",
    )(ap, dq, dkv.reshape(8, 4, 128, 128), wf, gf)
    layer, grad_q, grad_k, grad_v, grad_w = outs
    return (layer[None], grad_q[None], grad_k[None], grad_v[None], grad_w)


def solution(mesh):
    placed = (
        P("dp", "ctx", "tp"),
        P("dp", "ctx", "tp"),
        P("dp", "ctx", "tp"),
        P("ctx", "tp"),
        P("dp", "ctx", "tp"),
        P("dp", None, None),
    )
    return jax.shard_map(
        body,
        mesh=mesh,
        in_specs=placed,
        out_specs=(
            P("dp", "ctx", "tp"),
            P("dp", "ctx", "tp"),
            P("dp", "ctx", "tp"),
            P("dp", "ctx", "tp"),
            P("ctx", "tp"),
        ),
        check_vma=False,
    )
```

```python
import functools

import jax
import jax.numpy as jnp
from jax import lax
from jax.experimental import pallas as pl
from jax.experimental.pallas import tpu as pltpu
from jax.sharding import PartitionSpec as P

MESH = pl.DeviceIdType.MESH
HS = 64
NEG_FILL = -1e30
TILE = 512
CHUNK = 128
BF = jnp.bfloat16
F32 = jnp.float32
VMEM_LIMIT = 56 * 2**20
W_HALF_STEP = 3
W_DONE_STEP = 5
PROJECT_STEP = 2
CORE_STEP = 4


def swap_halves(first, second):
    low = lax.broadcasted_iota(jnp.int32, first.shape, 1) < HS
    first, second = first.astype(F32), second.astype(F32)
    return (
        jnp.where(low, first, pltpu.roll(second, HS, 1)).astype(BF),
        jnp.where(low, pltpu.roll(first, HS, 1), second).astype(BF),
    )


def remote(src, dst, send_sem, recv_sem, device):
    return pltpu.make_async_remote_copy(
        src_ref=src,
        dst_ref=dst,
        send_sem=send_sem,
        recv_sem=recv_sem,
        device_id=device,
        device_id_type=MESH,
    )


def places():
    ctx = lax.axis_index("ctx")
    dp = lax.axis_index("dp")
    tp = lax.axis_index("tp")
    return ctx, ctx // 4, ctx % 4, dp // 2, dp % 2, tp


def greet(devices):
    barrier = pltpu.get_barrier_semaphore()
    for device in devices:
        pl.semaphore_signal(barrier, inc=1, device_id=device, device_id_type=MESH)
    return lambda: pl.semaphore_wait(barrier, len(devices))


def order(step):
    half = (step + 1) // 2
    return (step % 2) * half + (1 - step % 2) * ((8 - half) % 8)


def sublayer_kernel(
    seg_ref, q_ref, k_ref, v_ref, w_ref, g_ref,
    layer_ref, dq_in, dkv_in, gw_ref,
    kv_out, q_out, qh, kv, wf, gf, g_out, gh,
    reach_ref, query, grad, both, probs, tops, top, total, out, base, delta, grad_q, acc,
    a_out, a_in, dq_out, part, part_in, part_sum,
    tp_out, tp_in, wp, core_in, core_sum, y_in, y_sum, m_in, m_sum, s_in, piece,
    local_sem, w_s, w_r, q_s, q_r, kv_s, kv_r, fwd_s, fwd_r, wm_s, wm_r, wy_s, wy_r, gh_s, gh_r,
    a_s, a_r, part_s, part_r, dkv_s, dkv_r, dq_s, dq_r, y_s, y_r, m_s, m_r, s_s, s_r, d_s, d_r, one_s, one_r,
):
    ctx, spot, member, row, core, tp = places()
    near_first = [1, 7, 2, 6, 3, 5, 4]
    peer_spots = [(spot + i) % 8 for i in near_first]
    source_spots = [(spot + 8 - i) % 8 for i in near_first]
    peers = [{"ctx": s * 4 + member} for s in peer_spots]
    group = [{"ctx": spot * 4 + (member + i) % 4} for i in range(1, 4)]
    dp = row * 2 + core
    dp_devs = [{"dp": (dp + i) % 8} for i in range(1, 8)]
    y_devs = [{"dp": ((row + i) % 4) * 2 + core} for i in range(1, 4)]
    core_dev = {"dp": row * 2 + 1 - core}
    tp_dev = {"tp": 1 - tp}
    ready = greet(peers + group + dp_devs + [tp_dev])

    sent = []

    def send(*copy_args):
        copy = remote(*copy_args)
        copy.start()
        sent.append(copy)

    def got(dst, recv_sem):
        remote(dst, dst, one_s.at[0], recv_sem, core_dev).wait_recv()

    low = lax.broadcasted_iota(jnp.int32, (64, 128), 1) < HS

    w_rows = pl.ds(pl.multiple_of(core * 32, 32), 32)
    w_cols = pl.ds(pl.multiple_of(row * 128, 128), 128)
    w_piece = w_ref.at[w_rows, w_cols]
    own_w = pltpu.make_async_copy(w_piece, wf.at[spot, member, w_rows, w_cols], local_sem.at[0])
    own_g = pltpu.make_async_copy(g_ref, gf.at[tp], local_sem.at[1])
    own_w.start()
    own_g.start()
    for pair in range(4):
        cols = slice(pair * 128, (pair + 1) * 128)
        even, odd = swap_halves(k_ref[:, cols], v_ref[:, cols])
        kv_out[2 * pair] = even
        kv_out[2 * pair + 1] = odd
        even, odd = swap_halves(q_ref[:64, cols], q_ref[64:, cols])
        q_out[2 * pair] = even
        q_out[2 * pair + 1] = odd
    own_kv = pltpu.make_async_copy(kv_out.at[spot], kv.at[spot, member], local_sem.at[2])
    own_q = pltpu.make_async_copy(q_out.at[spot], qh.at[spot], local_sem.at[3])
    own_kv.start()
    own_q.start()
    ready()

    for i in range(7):
        send(w_piece, wf.at[spot, member, w_rows, w_cols], w_s.at[i], w_r.at[i], peers[i])
    for i in range(7):
        send(q_out.at[peer_spots[i]], qh.at[spot], q_s.at[i], q_r.at[i], peers[i])
    for i in range(7):
        send(kv_out.at[peer_spots[i]], kv.at[spot, member], kv_s.at[i], kv_r.at[spot], peers[i])
    send(g_ref, gf.at[tp], one_s.at[0], one_r.at[0], tp_dev)

    def forward_copies(t):
        return [
            remote(kv.at[t, member], kv.at[t, member], fwd_s.at[t * 3 + i], fwd_r.at[t * 3 + i], group[i])
            for i in range(3)
        ]

    own_kv.wait()
    for copy in forward_copies(spot):
        copy.start()

    def reach_of(position):
        reach = position
        for seg in range(5):
            start, length, flag = seg_ref[0, seg], seg_ref[1, seg], seg_ref[2, seg]
            inside = (position >= start) & (position < start + length) & (flag == 1)
            reach = jnp.where(inside, start + length - 1, reach)
        return reach

    for index in range(8):
        position = (4 * index + member) * 128 + lax.broadcasted_iota(jnp.int32, (128, 128), 0)
        reach_ref[index * 128:(index + 1) * 128, :] = reach_of(position) - lax.broadcasted_iota(
            jnp.int32, (128, 128), 1
        )
    top[...] = jnp.full_like(top, NEG_FILL)
    total[...] = jnp.zeros_like(total)
    out[...] = jnp.zeros_like(out)
    grad_q[...] = jnp.zeros_like(grad_q)

    own_w.wait()
    for i in range(7):
        got(wf.at[source_spots[i], member, w_rows, w_cols], w_r.at[i])
    w_slab = wf.at[:, member, w_rows, w_cols]
    for i in range(3):
        send(w_slab, w_slab, wm_s.at[i], wm_r.at[i], group[i])

    own_q.wait()
    for i in range(7):
        got(qh.at[source_spots[i]], q_r.at[i])
    for index in range(8):
        packed = qh[index].astype(F32) * HS ** -0.5
        query[index * 128:index * 128 + 64, :] = jnp.where(low, packed, 0.0).astype(BF)
        query[index * 128 + 64:(index + 1) * 128, :] = jnp.where(
            low, pltpu.roll(packed, HS, 1), 0.0
        ).astype(BF)

    def first_pair(t):
        return jnp.maximum(4 * t - 5 - member, 0) // 8

    def forward_tile(t):
        tile = kv[t].reshape(TILE, 128)

        def pair(index, carry):
            rows = pl.ds(pl.multiple_of(index * 256, 256), 256)
            scores = lax.dot_general(
                query[rows, :], tile, (((1,), (1,)), ((), ())), preferred_element_type=F32
            )
            reach = reach_ref[rows, :] - t * TILE
            parts = [
                jnp.where(reach >= c * CHUNK, scores[:, c * CHUNK:(c + 1) * CHUNK], NEG_FILL)
                for c in range(TILE // CHUNK)
            ]
            best = jnp.maximum(jnp.maximum(parts[0], parts[1]), jnp.maximum(parts[2], parts[3]))
            before = top[rows, :]
            now = jnp.maximum(before, jnp.max(best, axis=1, keepdims=True))
            shrink = jnp.exp(before - now)
            parts = [jnp.exp(p - now) for p in parts]
            total[rows, :] = total[rows, :] * shrink + ((parts[0] + parts[1]) + (parts[2] + parts[3]))
            low_probs = jnp.concatenate([p.astype(BF) for p in parts], axis=1)
            probs[t, rows, :] = low_probs
            out[rows, :] = out[rows, :] * shrink + jnp.dot(
                low_probs, tile, preferred_element_type=F32
            )
            top[rows, :] = now
            tops[t, rows, :] = now
            return carry

        lax.fori_loop(first_pair(t), 4, pair, 0)

    w_part = wf.at[:, :, w_rows, w_cols]
    w_half = wf.at[:, :, w_rows, :]

    def weight_copies():
        return [remote(w_part, w_part, wy_s.at[i], wy_r.at[i], y_devs[i]) for i in range(3)]

    def half_copy():
        return remote(w_half, w_half, one_s.at[1], one_r.at[1], core_dev)

    def grad_copies():
        return [
            remote(g_out.at[peer_spots[i]], gh.at[spot], gh_s.at[i], gh_r.at[i], peers[i])
            for i in range(7)
        ]

    own_gh = pltpu.make_async_copy(g_out.at[spot], gh.at[spot], local_sem.at[4])

    def forward_step(step, carry):
        t = (spot + order(step)) % 8

        @pl.when(step < 7)
        def _():
            later = (spot + order(step + 1)) % 8
            got(kv.at[later, member], kv_r.at[later])
            for copy in forward_copies(later):
                copy.start()

        for i in range(3):
            got(kv.at[t, (member + 3 - i) % 4], fwd_r.at[t * 3 + i])
        forward_tile(t)

        @pl.when(step == 0)
        def _():
            for i in range(3):
                got(wf.at[:, (member + 3 - i) % 4, w_rows, w_cols], wm_r.at[i])
            for copy in weight_copies():
                copy.start()

        @pl.when(step == W_HALF_STEP)
        def _():
            for i in range(3):
                from_row = (row + 3 - i) % 4
                got(wf.at[:, :, w_rows, pl.ds(pl.multiple_of(from_row * 128, 128), 128)], wy_r.at[i])
            half_copy().start()

        @pl.when(step == W_DONE_STEP)
        def _():
            got(wf.at[:, :, pl.ds(pl.multiple_of(32 - core * 32, 32), 32), :], one_r.at[1])
            own_g.wait()
            got(gf.at[1 - tp], one_r.at[0])
            weight = wf[...].reshape(2048, 512)
            grad_attn = jnp.dot(gf[0], weight[:1024], preferred_element_type=F32)
            grad_attn += jnp.dot(gf[1], weight[1024:], preferred_element_type=F32)
            grad_attn = grad_attn.astype(BF)
            for two in range(4):
                cols = slice(two * 128, (two + 1) * 128)
                even, odd = swap_halves(grad_attn[:64, cols], grad_attn[64:, cols])
                g_out[2 * two] = even
                g_out[2 * two + 1] = odd
            own_gh.start()
            for copy in grad_copies():
                copy.start()

        return carry

    lax.fori_loop(0, 8, forward_step, 0)

    def finish(index, carry):
        rows = pl.ds(pl.multiple_of(index * 128, 128), 128)
        row_sum = jnp.sum(total[rows, :], axis=1, keepdims=True)
        values = (out[rows, :] * (1.0 / row_sum)).astype(BF).astype(F32)
        out[rows, :] = values
        base[rows, :] = top[rows, :] + jnp.log(row_sum)
        a_out[index] = jnp.where(low, pltpu.roll(values[:64], HS, 1), values[64:]).astype(BF)
        return carry

    lax.fori_loop(0, 8, finish, 0)
    own_a = pltpu.make_async_copy(a_out.at[spot], a_in.at[spot], local_sem.at[5])
    own_a.start()
    for i in range(7):
        send(a_out.at[peer_spots[i]], a_in.at[spot], a_s.at[i], a_r.at[i], peers[i])

    own_gh.wait()
    for i in range(7):
        got(gh.at[source_spots[i]], gh_r.at[i])

    def spread(index, carry):
        rows = pl.ds(pl.multiple_of(index * 128, 128), 128)
        packed = gh[index].astype(F32)
        values = jnp.concatenate(
            [jnp.where(low, 0.0, pltpu.roll(packed, HS, 1)), jnp.where(low, 0.0, packed)], axis=0
        )
        grad[rows, :] = values.astype(BF)
        both[rows, :] = query[rows, :].astype(F32) + values
        delta[rows, :] = jnp.broadcast_to(
            jnp.sum(values * out[rows, :], axis=1, keepdims=True), (128, 128)
        )
        return carry

    lax.fori_loop(0, 8, spread, 0)

    def backward_tile(t):
        tile = kv[t].reshape(TILE, 128)
        acc[...] = jnp.zeros_like(acc)

        def pair(index, carry):
            rows = pl.ds(pl.multiple_of(index * 256, 256), 256)
            factor = jnp.exp(tops[t, rows, :] - base[rows, :])
            turned = jnp.transpose(both[rows, :] * factor).astype(BF)
            grad_probs = lax.dot_general(
                grad[rows, :], tile, (((1,), (1,)), ((), ())), preferred_element_type=F32
            )
            low_probs = probs[t, rows, :]
            shift = delta[rows, :]
            grad_scores = jnp.concatenate(
                [
                    (
                        low_probs[:, c * CHUNK:(c + 1) * CHUNK].astype(F32)
                        * (grad_probs[:, c * CHUNK:(c + 1) * CHUNK] - shift)
                    ).astype(BF)
                    for c in range(TILE // CHUNK)
                ],
                axis=1,
            )
            acc[:HS, :] += jnp.dot(turned[:HS], grad_scores, preferred_element_type=F32)
            acc[HS:, :] += jnp.dot(turned[HS:], low_probs, preferred_element_type=F32)
            grad_q[rows, :] += factor * jnp.dot(grad_scores, tile, preferred_element_type=F32)
            return carry

        lax.fori_loop(first_pair(t), 4, pair, 0)
        part[t] = jnp.transpose(acc[...]).astype(BF).reshape(4, 128, 128)

    def part_copies(t):
        return [
            remote(part.at[t, (member + i + 1) % 4], part_in.at[t, i], part_s.at[t * 3 + i], part_r.at[t * 3 + i], group[i])
            for i in range(3)
        ]

    def home_copy(t):
        return remote(part_sum.at[t], dkv_in.at[spot], dkv_s.at[t], dkv_r.at[spot], {"ctx": t * 4 + member})

    own_dkv = pltpu.make_async_copy(part_sum.at[spot], dkv_in.at[spot], local_sem.at[6])

    def send_home(t):
        for i in range(3):
            got(part_in.at[t, i], part_r.at[t * 3 + i])
        part_sum[t] = (
            (part[t, member].astype(F32) + part_in[t, 0].astype(F32))
            + (part_in[t, 1].astype(F32) + part_in[t, 2].astype(F32))
        ).astype(BF)

    def core_copy():
        return remote(wp.at[:, :, 1 - core], core_in, one_s.at[2], one_r.at[2], core_dev)

    def tp_copy():
        return remote(tp_out.at[1 - tp], tp_in, one_s.at[3], one_r.at[3], tp_dev)

    def y_copies():
        return [
            remote(
                core_sum.at[:, :, :, pl.ds(pl.multiple_of(((row + i + 1) % 4) * 128, 128), 128)],
                y_in.at[i], y_s.at[i], y_r.at[i], y_devs[i],
            )
            for i in range(3)
        ]

    def project():
        own_a.wait()
        for i in range(7):
            got(a_in.at[source_spots[i]], a_r.at[i])
        uppers, lowers = [], []
        for two in range(4):
            upper, lower = swap_halves(a_in[2 * two], a_in[2 * two + 1])
            uppers.append(upper)
            lowers.append(lower)
        attn = jnp.concatenate(
            [jnp.concatenate(uppers, axis=1), jnp.concatenate(lowers, axis=1)], axis=0
        )
        for half in range(2):
            share = lax.dot_general(
                gf[half], attn, (((0,), (0,)), ((), ())), preferred_element_type=F32
            )
            wp[half * 4:(half + 1) * 4] = share.astype(BF).reshape(4, 4, 2, 32, 512)
        core_copy().start()
        weight = wf[...].reshape(2, 1024, 512)
        for half in range(2):
            share = lax.dot_general(
                attn, weight[half], (((1,), (1,)), ((), ())), preferred_element_type=F32
            )
            tp_out[half] = share.astype(BF)
        tp_copy().start()

    def add_core():
        got(core_in, one_r.at[2])
        core_sum[...] = (wp[:, :, core].astype(F32) + core_in[...].astype(F32)).astype(BF)
        for copy in y_copies():
            copy.start()

    def backward_step(step, carry):
        t = (spot + order(7 - step)) % 8
        backward_tile(t)
        for copy in part_copies(t):
            copy.start()

        @pl.when(step > 0)
        def _():
            earlier = (spot + order(8 - step)) % 8
            send_home(earlier)
            home_copy(earlier).start()

        @pl.when(step == PROJECT_STEP)
        def _():
            project()

        @pl.when(step == CORE_STEP)
        def _():
            add_core()

        return carry

    lax.fori_loop(0, 8, backward_step, 0)

    def pack_query(index, carry):
        rows = pl.ds(pl.multiple_of(index * 128, 128), 128)
        values = grad_q[rows, :] * HS ** -0.5
        dq_out[index] = jnp.where(low, values[:64], pltpu.roll(values[64:], HS, 1)).astype(BF)
        return carry

    lax.fori_loop(0, 8, pack_query, 0)
    own_dq = pltpu.make_async_copy(dq_out.at[spot], dq_in.at[spot], local_sem.at[7])
    own_dq.start()
    for i in range(7):
        send(dq_out.at[peer_spots[i]], dq_in.at[spot], dq_s.at[i], dq_r.at[i], peers[i])
    send_home(spot)
    own_dkv.start()

    got(tp_in, one_r.at[3])
    layer_ref[...] = (tp_out[tp].astype(F32) + tp_in[...].astype(F32)).astype(BF)

    for i in range(3):
        got(y_in.at[i], y_r.at[i])
    y_sum[...] = (
        (core_sum[:, :, :, w_cols].astype(F32) + y_in[0].astype(F32))
        + (y_in[1].astype(F32) + y_in[2].astype(F32))
    ).astype(BF)
    for i in range(3):
        send(y_sum.at[:, (member + i + 1) % 4], m_in.at[i], m_s.at[i], m_r.at[i], group[i])
    for i in range(3):
        got(m_in.at[i], m_r.at[i])
    m_sum[...] = (
        (y_sum[:, member].astype(F32) + m_in[0].astype(F32))
        + (m_in[1].astype(F32) + m_in[2].astype(F32))
    ).astype(BF)
    for i in range(7):
        send(m_sum.at[peer_spots[i]], s_in.at[i], s_s.at[i], s_r.at[i], peers[i])
    summed = m_sum[spot].astype(F32)
    for i in range(7):
        got(s_in.at[i], s_r.at[i])
        summed = summed + s_in[i].astype(F32)
    piece[...] = summed
    own_spot = gw_ref.at[w_rows, w_cols]
    own_piece = pltpu.make_async_copy(piece, own_spot, local_sem.at[8])
    own_piece.start()
    for i in range(7):
        send(piece, own_spot, d_s.at[i], d_r.at[i], dp_devs[i])

    own_dq.wait()
    own_dkv.wait()
    for i in range(7):
        got(dq_in.at[source_spots[i]], dq_r.at[i])
        got(dkv_in.at[source_spots[i]], dkv_r.at[source_spots[i]])
    own_piece.wait()
    for i in range(7):
        source = (dp + 7 - i) % 8
        got(
            gw_ref.at[
                pl.ds(pl.multiple_of((source % 2) * 32, 32), 32),
                pl.ds(pl.multiple_of((source // 2) * 128, 128), 128),
            ],
            d_r.at[i],
        )

    def settle(t, carry):
        for copy in forward_copies(t) + part_copies(t):
            copy.wait_send()

        @pl.when(t != spot)
        def _():
            home_copy(t).wait_send()

        return carry

    lax.fori_loop(0, 8, settle, 0)
    for copy in weight_copies() + grad_copies() + y_copies() + [half_copy(), core_copy(), tp_copy()]:
        copy.wait_send()
    for copy in sent:
        copy.wait_send()


def finish_kernel(layer_in, dq_in, dkv_in, gw_in, layer_ref, gq_ref, gk_ref, gv_ref, gw_ref):
    layer_ref[...] = layer_in[...]
    gw_ref[...] = gw_in[...]
    for pair in range(4):
        cols = slice(pair * 128, (pair + 1) * 128)
        upper, lower = swap_halves(dq_in[2 * pair], dq_in[2 * pair + 1])
        gq_ref[:64, cols] = upper
        gq_ref[64:, cols] = lower
        keys, values = swap_halves(dkv_in[2 * pair], dkv_in[2 * pair + 1])
        gk_ref[:, cols] = keys
        gv_ref[:, cols] = values


def like(shape, dtype=BF):
    return jax.ShapeDtypeStruct(shape, dtype)


def dma(*counts):
    return [pltpu.SemaphoreType.DMA((count,)) for count in counts]


def body(query_states, key_states, value_states, out_weight, grad_output, segment_table):
    vmem = pl.BlockSpec(memory_space=pltpu.VMEM)
    smem = pl.BlockSpec(memory_space=pltpu.SMEM)
    low = lambda *shape: pltpu.VMEM(shape, BF)
    wide = lambda *shape: pltpu.VMEM(shape, F32)
    layer, dq, dkv, gw = pl.pallas_call(
        sublayer_kernel,
        out_shape=(like((128, 1024)), like((8, 64, 128)), like((8, 128, 128)), like((64, 512), F32)),
        in_specs=[smem] + [vmem] * 5,
        out_specs=(vmem,) * 4,
        scratch_shapes=[
            low(8, 128, 128), low(8, 64, 128), low(8, 64, 128), low(8, 4, 128, 128),
            low(8, 4, 64, 512), low(2, 128, 1024), low(8, 64, 128), low(8, 64, 128),
            pltpu.VMEM((1024, 128), jnp.int32), low(1024, 128), low(1024, 128), wide(1024, 128),
            low(8, 1024, 512), wide(8, 1024, 128), wide(1024, 128), wide(1024, 128), wide(1024, 128),
            wide(1024, 128), wide(1024, 128), wide(1024, 128), wide(128, 512),
            low(8, 64, 128), low(8, 64, 128), low(8, 64, 128),
            low(8, 4, 128, 128), low(8, 3, 128, 128), low(8, 128, 128),
            low(2, 128, 1024), low(128, 1024), low(8, 4, 2, 32, 512), low(8, 4, 32, 512),
            low(8, 4, 32, 512), low(3, 8, 4, 32, 128), low(8, 4, 32, 128), low(3, 8, 32, 128),
            low(8, 32, 128), low(7, 32, 128), wide(32, 128),
            *dma(9, 7, 7, 7, 7, 7, 8, 24, 24, 3, 3, 3, 3, 7, 7),
            *dma(7, 7, 24, 24, 8, 8, 7, 7, 3, 3, 3, 3, 7, 7, 7, 7, 4, 4),
        ],
        compiler_params=pltpu.CompilerParams(
            collective_id=0, has_side_effects=True, vmem_limit_bytes=VMEM_LIMIT
        ),
        name="sublayer",
    )(
        segment_table[0], query_states[0], key_states[0], value_states[0], out_weight, grad_output[0]
    )
    outs = pl.pallas_call(
        finish_kernel,
        out_shape=(
            like((128, 1024)), like((128, 512)), like((128, 512)), like((128, 512)), like((64, 512), F32),
        ),
        in_specs=[vmem] * 4,
        out_specs=(vmem,) * 5,
        name="unpack",
    )(layer, dq, dkv, gw)
    layer, grad_q, grad_k, grad_v, grad_w = outs
    return (layer[None], grad_q[None], grad_k[None], grad_v[None], grad_w)


def solution(mesh):
    placed = (
        P("dp", "ctx", "tp"),
        P("dp", "ctx", "tp"),
        P("dp", "ctx", "tp"),
        P("ctx", "tp"),
        P("dp", "ctx", "tp"),
        P("dp", None, None),
    )
    return jax.shard_map(
        body,
        mesh=mesh,
        in_specs=placed,
        out_specs=(
            P("dp", "ctx", "tp"),
            P("dp", "ctx", "tp"),
            P("dp", "ctx", "tp"),
            P("dp", "ctx", "tp"),
            P("ctx", "tp"),
        ),
        check_vma=False,
    )
```

```python
import functools

import jax
import jax.numpy as jnp
from jax import lax
from jax.experimental import pallas as pl
from jax.experimental.pallas import tpu as pltpu
from jax.sharding import PartitionSpec as P

MESH = pl.DeviceIdType.MESH
HS = 64
NEG_FILL = -1e30
TILE = 512
CHUNK = 128
BF = jnp.bfloat16
F32 = jnp.float32
VMEM_LIMIT = 56 * 2**20
FORWARD_ROWS = 1024
BACKWARD_ROWS = 512
AHEAD = 4
RELAY = 2
BEHIND = 2
BEHIND_Z = 3
SWAP_STEP = 4
W_HALF_STEP = 6
CORE_STEP = 0
ROW_STEP = 4


def swap_halves(first, second):
    low = lax.broadcasted_iota(jnp.int32, first.shape, 1) < HS
    first, second = first.astype(F32), second.astype(F32)
    return (
        jnp.where(low, first, pltpu.roll(second, HS, 1)).astype(BF),
        jnp.where(low, pltpu.roll(first, HS, 1), second).astype(BF),
    )


def remote(src, dst, send_sem, recv_sem, device):
    return pltpu.make_async_remote_copy(
        src_ref=src,
        dst_ref=dst,
        send_sem=send_sem,
        recv_sem=recv_sem,
        device_id=device,
        device_id_type=MESH,
    )


def places():
    ctx = lax.axis_index("ctx")
    dp = lax.axis_index("dp")
    tp = lax.axis_index("tp")
    return ctx, ctx // 4, ctx % 4, dp // 2, dp % 2, tp


def flip_x(member):
    return member + 1 - 2 * (member % 2)


def flip_z(member):
    return member + 2 - 4 * (member // 2)


def greet(devices):
    barrier = pltpu.get_barrier_semaphore()
    for device in devices:
        pl.semaphore_signal(barrier, inc=1, device_id=device, device_id_type=MESH)
    return lambda: pl.semaphore_wait(barrier, len(devices))


def order(step):
    half = (step + 1) // 2
    return (step % 2) * half + (1 - step % 2) * ((8 - half) % 8)


def sublayer_kernel(
    seg_ref, q_ref, k_ref, v_ref, w_ref, g_ref,
    layer_ref, dq_in, dkv_in, gw_ref,
    kv_out, q_out, qh, kv, wf, gf, g_out, gh,
    reach_ref, query, grad, both, probs, tops, top, total, out, base, delta, grad_q, acc,
    a_out, a_in, dq_out, part, part_in, part_sum, part_all,
    tp_out, tp_in, wp, core_in, core_sum, y_in, y_sum, m_in, m_sum, s_in, piece,
    local_sem, w_s, w_r, q_s, q_r, kv_s, kv_r, fwd_s, fwd_r, wm_s, wm_r, wy_s, wy_r, gh_s, gh_r,
    a_s, a_r, part_s, part_r, dkv_s, dkv_r, dq_s, dq_r, y_s, y_r, m_s, m_r, s_s, s_r, d_s, d_r, core_s, core_r, one_s, one_r,
):
    ctx, spot, member, row, core, tp = places()
    near_first = [1, 7, 2, 6, 3, 5, 4]
    peer_spots = [(spot + i) % 8 for i in near_first]
    source_spots = [(spot + 8 - i) % 8 for i in near_first]
    peers = [{"ctx": s * 4 + member} for s in peer_spots]
    group = [{"ctx": spot * 4 + (member + i) % 4} for i in range(1, 4)]
    dp = row * 2 + core
    dp_devs = [{"dp": (dp + i) % 8} for i in range(1, 8)]
    y_devs = [{"dp": ((row + i) % 4) * 2 + core} for i in range(1, 4)]
    core_dev = {"dp": row * 2 + 1 - core}
    tp_dev = {"tp": 1 - tp}
    ready = greet(peers + group + dp_devs + [tp_dev])

    sent = []

    def send(*copy_args):
        copy = remote(*copy_args)
        copy.start()
        sent.append(copy)

    def got(dst, recv_sem):
        remote(dst, dst, one_s.at[0], recv_sem, core_dev).wait_recv()

    low = lax.broadcasted_iota(jnp.int32, (64, 128), 1) < HS

    w_rows = pl.ds(pl.multiple_of(core * 32, 32), 32)
    w_cols = pl.ds(pl.multiple_of(row * 128, 128), 128)
    w_piece = w_ref.at[w_rows, w_cols]
    own_w = pltpu.make_async_copy(w_piece, wf.at[spot, member, w_rows, w_cols], local_sem.at[0])
    own_g = pltpu.make_async_copy(g_ref, gf.at[tp], local_sem.at[1])
    own_w.start()
    own_g.start()
    for pair in range(4):
        cols = slice(pair * 128, (pair + 1) * 128)
        even, odd = swap_halves(k_ref[:, cols], v_ref[:, cols])
        kv_out[2 * pair] = even
        kv_out[2 * pair + 1] = odd
        even, odd = swap_halves(q_ref[:64, cols], q_ref[64:, cols])
        q_out[2 * pair] = even
        q_out[2 * pair + 1] = odd
    own_kv = pltpu.make_async_copy(kv_out.at[spot], kv.at[spot, member], local_sem.at[2])
    own_q = pltpu.make_async_copy(q_out.at[spot], qh.at[spot], local_sem.at[3])
    own_kv.start()
    own_q.start()
    ready()

    for i in range(7):
        send(w_piece, wf.at[spot, member, w_rows, w_cols], w_s.at[i], w_r.at[i], peers[i])
    for i in range(7):
        send(q_out.at[peer_spots[i]], qh.at[spot], q_s.at[i], q_r.at[i], peers[i])
    for i in range(7):
        send(kv_out.at[peer_spots[i]], kv.at[spot, member], kv_s.at[i], kv_r.at[spot], peers[i])

    x_member, z_member = flip_x(member), flip_z(member)
    x_dev = {"ctx": spot * 4 + x_member}
    z_dev = {"ctx": spot * 4 + z_member}

    def share_copy(t, which, i, device):
        slab = kv.at[t, which]
        return remote(slab, slab, fwd_s.at[t * 3 + i], fwd_r.at[t * 3 + i], device)

    def forward_copies(t):
        return [share_copy(t, member, 0, z_dev), share_copy(t, member, 1, x_dev)]

    def relay_copy(t):
        return share_copy(t, z_member, 2, x_dev)

    own_kv.wait()
    for copy in forward_copies(spot):
        copy.start()

    def reach_of(position):
        reach = position
        for seg in range(5):
            start, length, flag = seg_ref[0, seg], seg_ref[1, seg], seg_ref[2, seg]
            inside = (position >= start) & (position < start + length) & (flag == 1)
            reach = jnp.where(inside, start + length - 1, reach)
        return reach

    for index in range(8):
        position = (4 * index + member) * 128 + lax.broadcasted_iota(jnp.int32, (128, 128), 0)
        reach_ref[index * 128:(index + 1) * 128, :] = reach_of(position) - lax.broadcasted_iota(
            jnp.int32, (128, 128), 1
        )
    top[...] = jnp.full_like(top, NEG_FILL)
    total[...] = jnp.zeros_like(total)
    out[...] = jnp.zeros_like(out)
    grad_q[...] = jnp.zeros_like(grad_q)

    own_w.wait()
    for i in range(7):
        got(wf.at[source_spots[i], member, w_rows, w_cols], w_r.at[i])
    w_slab = wf.at[:, member, w_rows, w_cols]
    for i in range(3):
        send(w_slab, w_slab, wm_s.at[i], wm_r.at[i], group[i])

    own_q.wait()
    for i in range(7):
        got(qh.at[source_spots[i]], q_r.at[i])
    for index in range(8):
        packed = qh[index].astype(F32) * HS ** -0.5
        query[index * 128:index * 128 + 64, :] = jnp.where(low, packed, 0.0).astype(BF)
        query[index * 128 + 64:(index + 1) * 128, :] = jnp.where(
            low, pltpu.roll(packed, HS, 1), 0.0
        ).astype(BF)

    def first_group(t, row_count):
        return jnp.maximum(4 * t - 5 - member, 0) // (row_count // 32)

    def forward_tile(t):
        tile = kv[t].reshape(TILE, 128)

        def group_of(index, carry):
            rows = pl.ds(pl.multiple_of(index * FORWARD_ROWS, FORWARD_ROWS), FORWARD_ROWS)
            scores = lax.dot_general(
                query[rows, :], tile, (((1,), (1,)), ((), ())), preferred_element_type=F32
            )
            reach = reach_ref[rows, :] - t * TILE
            parts = [
                jnp.where(reach >= c * CHUNK, scores[:, c * CHUNK:(c + 1) * CHUNK], NEG_FILL)
                for c in range(TILE // CHUNK)
            ]
            best = jnp.maximum(jnp.maximum(parts[0], parts[1]), jnp.maximum(parts[2], parts[3]))
            before = top[rows, :]
            now = jnp.maximum(before, jnp.max(best, axis=1, keepdims=True))
            shrink = jnp.exp(before - now)
            parts = [jnp.exp(p - now) for p in parts]
            total[rows, :] = total[rows, :] * shrink + ((parts[0] + parts[1]) + (parts[2] + parts[3]))
            low_probs = jnp.concatenate([p.astype(BF) for p in parts], axis=1)
            probs[t, rows, :] = low_probs
            out[rows, :] = out[rows, :] * shrink + jnp.dot(
                low_probs, tile, preferred_element_type=F32
            )
            top[rows, :] = now
            tops[t, rows, :] = now
            return carry

        lax.fori_loop(first_group(t, FORWARD_ROWS), 1024 // FORWARD_ROWS, group_of, 0)

    w_part = wf.at[:, :, w_rows, w_cols]
    w_half = wf.at[:, :, w_rows, :]

    def weight_copies():
        return [remote(w_part, w_part, wy_s.at[i], wy_r.at[i], y_devs[i]) for i in range(3)]

    def half_copy():
        return remote(w_half, w_half, one_s.at[1], one_r.at[1], core_dev)

    def grad_copies():
        return [
            remote(g_out.at[peer_spots[i]], gh.at[spot], gh_s.at[i], gh_r.at[i], peers[i])
            for i in range(7)
        ]

    def swap_copy():
        return remote(g_ref, gf.at[tp], one_s.at[0], one_r.at[0], tp_dev)

    own_gh = pltpu.make_async_copy(g_out.at[spot], gh.at[spot], local_sem.at[4])

    def pass_on(step):
        t = (spot + order(step)) % 8
        got(kv.at[t, member], kv_r.at[t])
        for copy in forward_copies(t):
            copy.start()

    def forward_step(step, carry):
        t = (spot + order(step)) % 8

        @pl.when(step < 8 - AHEAD)
        def _():
            pass_on(step + AHEAD)

        @pl.when(step < 8 - RELAY)
        def _():
            relay(step + RELAY)

        got(kv.at[t, x_member], fwd_r.at[t * 3 + 1])
        got(kv.at[t, flip_z(x_member)], fwd_r.at[t * 3 + 2])
        forward_tile(t)

        @pl.when(step == 0)
        def _():
            for i in range(3):
                got(wf.at[:, (member + 3 - i) % 4, w_rows, w_cols], wm_r.at[i])
            for copy in weight_copies():
                copy.start()

        @pl.when(step == W_HALF_STEP)
        def _():
            for i in range(3):
                from_row = (row + 3 - i) % 4
                got(wf.at[:, :, w_rows, pl.ds(pl.multiple_of(from_row * 128, 128), 128)], wy_r.at[i])
            half_copy().start()

        @pl.when(step == SWAP_STEP)
        def _():
            swap_copy().start()

        return carry

    def relay(step):
        t = (spot + order(step)) % 8
        got(kv.at[t, z_member], fwd_r.at[t * 3])
        relay_copy(t).start()

    for step in range(1, AHEAD):
        pass_on(step)
    for step in range(RELAY):
        relay(step)
    lax.fori_loop(0, 8, forward_step, 0)

    def finish(index, carry):
        rows = pl.ds(pl.multiple_of(index * 128, 128), 128)
        row_sum = jnp.sum(total[rows, :], axis=1, keepdims=True)
        values = (out[rows, :] * (1.0 / row_sum)).astype(BF).astype(F32)
        out[rows, :] = values
        base[rows, :] = top[rows, :] + jnp.log(row_sum)
        a_out[index] = jnp.where(low, pltpu.roll(values[:64], HS, 1), values[64:]).astype(BF)
        return carry

    lax.fori_loop(0, 8, finish, 0)
    own_a = pltpu.make_async_copy(a_out.at[spot], a_in.at[spot], local_sem.at[5])
    own_a.start()
    for i in range(7):
        send(a_out.at[peer_spots[i]], a_in.at[spot], a_s.at[i], a_r.at[i], peers[i])

    got(wf.at[:, :, pl.ds(pl.multiple_of(32 - core * 32, 32), 32), :], one_r.at[1])
    own_g.wait()
    got(gf.at[1 - tp], one_r.at[0])
    weight = wf[...].reshape(2048, 512)
    grad_attn = jnp.dot(gf[0], weight[:1024], preferred_element_type=F32)
    grad_attn += jnp.dot(gf[1], weight[1024:], preferred_element_type=F32)
    grad_attn = grad_attn.astype(BF)
    for two in range(4):
        cols = slice(two * 128, (two + 1) * 128)
        even, odd = swap_halves(grad_attn[:64, cols], grad_attn[64:, cols])
        g_out[2 * two] = even
        g_out[2 * two + 1] = odd
    own_gh.start()
    for copy in grad_copies():
        copy.start()

    def core_copy(half):
        spots = pl.ds(half * 4, 4)
        return remote(
            wp.at[spots, :, 1 - core], core_in.at[spots], core_s.at[half], core_r.at[half], core_dev
        )

    def tp_copy():
        return remote(tp_out.at[1 - tp], tp_in, one_s.at[3], one_r.at[3], tp_dev)

    def y_copies(half):
        spots = pl.ds(half * 4, 4)
        return [
            remote(
                core_sum.at[spots, :, :, pl.ds(pl.multiple_of(((row + i + 1) % 4) * 128, 128), 128)],
                y_in.at[i, spots], y_s.at[half * 3 + i], y_r.at[half * 3 + i], y_devs[i],
            )
            for i in range(3)
        ]

    def project():
        own_a.wait()
        for i in range(7):
            got(a_in.at[source_spots[i]], a_r.at[i])
        uppers, lowers = [], []
        for two in range(4):
            upper, lower = swap_halves(a_in[2 * two], a_in[2 * two + 1])
            uppers.append(upper)
            lowers.append(lower)
        attn = jnp.concatenate(
            [jnp.concatenate(uppers, axis=1), jnp.concatenate(lowers, axis=1)], axis=0
        )
        for half in range(2):
            share = lax.dot_general(
                gf[half], attn, (((0,), (0,)), ((), ())), preferred_element_type=F32
            )
            wp[half * 4:(half + 1) * 4] = share.astype(BF).reshape(4, 4, 2, 32, 512)
            core_copy(half).start()
        weight = wf[...].reshape(2, 1024, 512)
        for half in range(2):
            share = lax.dot_general(
                attn, weight[half], (((1,), (1,)), ((), ())), preferred_element_type=F32
            )
            tp_out[half] = share.astype(BF)
        tp_copy().start()

    def add_core():
        for half in range(2):
            spots = pl.ds(half * 4, 4)
            got(core_in.at[spots], core_r.at[half])
            core_sum[spots] = (wp[spots, :, core].astype(F32) + core_in[spots].astype(F32)).astype(BF)
            for copy in y_copies(half):
                copy.start()

    project()

    own_gh.wait()
    for i in range(7):
        got(gh.at[source_spots[i]], gh_r.at[i])

    def spread(index, carry):
        rows = pl.ds(pl.multiple_of(index * 128, 128), 128)
        packed = gh[index].astype(F32)
        values = jnp.concatenate(
            [jnp.where(low, 0.0, pltpu.roll(packed, HS, 1)), jnp.where(low, 0.0, packed)], axis=0
        )
        grad[rows, :] = values.astype(BF)
        both[rows, :] = query[rows, :].astype(F32) + values
        delta[rows, :] = jnp.broadcast_to(
            jnp.sum(values * out[rows, :], axis=1, keepdims=True), (128, 128)
        )
        return carry

    lax.fori_loop(0, 8, spread, 0)

    def backward_tile(t):
        tile = kv[t].reshape(TILE, 128)
        acc[...] = jnp.zeros_like(acc)

        def group_of(index, carry):
            rows = pl.ds(pl.multiple_of(index * BACKWARD_ROWS, BACKWARD_ROWS), BACKWARD_ROWS)
            factor = jnp.exp(tops[t, rows, :] - base[rows, :])
            turned = jnp.transpose(both[rows, :] * factor).astype(BF)
            grad_probs = lax.dot_general(
                grad[rows, :], tile, (((1,), (1,)), ((), ())), preferred_element_type=F32
            )
            low_probs = probs[t, rows, :]
            shift = delta[rows, :]
            grad_scores = jnp.concatenate(
                [
                    (
                        low_probs[:, c * CHUNK:(c + 1) * CHUNK].astype(F32)
                        * (grad_probs[:, c * CHUNK:(c + 1) * CHUNK] - shift)
                    ).astype(BF)
                    for c in range(TILE // CHUNK)
                ],
                axis=1,
            )
            acc[:HS, :] += jnp.dot(turned[:HS], grad_scores, preferred_element_type=F32)
            acc[HS:, :] += jnp.dot(turned[HS:], low_probs, preferred_element_type=F32)
            grad_q[rows, :] += factor * jnp.dot(grad_scores, tile, preferred_element_type=F32)
            return carry

        lax.fori_loop(first_group(t, BACKWARD_ROWS), 1024 // BACKWARD_ROWS, group_of, 0)
        part[t] = jnp.transpose(acc[...]).astype(BF).reshape(4, 128, 128)

    def part_copies(t):
        return [
            remote(part.at[t, x_member], part_in.at[t, 0], part_s.at[t * 3], part_r.at[t * 3], x_dev),
            remote(
                part.at[t, flip_z(x_member)], part_in.at[t, 1],
                part_s.at[t * 3 + 1], part_r.at[t * 3 + 1], x_dev,
            ),
        ]

    def part_z_copy(t):
        return remote(
            part_sum.at[t], part_in.at[t, 2], part_s.at[t * 3 + 2], part_r.at[t * 3 + 2], z_dev
        )

    def home_copy(t):
        return remote(part_all.at[t], dkv_in.at[spot], dkv_s.at[t], dkv_r.at[spot], {"ctx": t * 4 + member})

    own_dkv = pltpu.make_async_copy(part_all.at[spot], dkv_in.at[spot], local_sem.at[6])

    def send_z(t):
        for i in range(2):
            got(part_in.at[t, i], part_r.at[t * 3 + i])
        part_sum[t] = (part[t, z_member].astype(F32) + part_in[t, 1].astype(F32)).astype(BF)
        part_z_copy(t).start()

    def send_home(t):
        got(part_in.at[t, 2], part_r.at[t * 3 + 2])
        part_all[t] = (
            part[t, member].astype(F32) + part_in[t, 0].astype(F32) + part_in[t, 2].astype(F32)
        ).astype(BF)

    def group_copies():
        return [
            remote(y_sum.at[:, (member + i + 1) % 4], m_in.at[i], m_s.at[i], m_r.at[i], group[i])
            for i in range(3)
        ]

    def add_rows():
        for half in range(2):
            for i in range(3):
                got(y_in.at[i, pl.ds(half * 4, 4)], y_r.at[half * 3 + i])
        y_sum[...] = (
            (core_sum[:, :, :, w_cols].astype(F32) + y_in[0].astype(F32))
            + (y_in[1].astype(F32) + y_in[2].astype(F32))
        ).astype(BF)
        for copy in group_copies():
            copy.start()

    def backward_step(step, carry):
        t = (spot + order(7 - step)) % 8
        backward_tile(t)
        for copy in part_copies(t):
            copy.start()

        @pl.when(step >= BEHIND)
        def _():
            send_z((spot + order(7 + BEHIND - step)) % 8)

        @pl.when(step >= BEHIND_Z)
        def _():
            earlier = (spot + order(7 + BEHIND_Z - step)) % 8
            send_home(earlier)
            home_copy(earlier).start()

        @pl.when(step == CORE_STEP)
        def _():
            add_core()

        @pl.when(step == ROW_STEP)
        def _():
            add_rows()

        return carry

    lax.fori_loop(0, 8, backward_step, 0)

    for i in range(3):
        got(m_in.at[i], m_r.at[i])
    m_sum[...] = (
        (y_sum[:, member].astype(F32) + m_in[0].astype(F32))
        + (m_in[1].astype(F32) + m_in[2].astype(F32))
    ).astype(BF)
    for i in range(7):
        send(m_sum.at[peer_spots[i]], s_in.at[i], s_s.at[i], s_r.at[i], peers[i])
    def pack_query(index, carry):
        rows = pl.ds(pl.multiple_of(index * 128, 128), 128)
        values = grad_q[rows, :] * HS ** -0.5
        dq_out[index] = jnp.where(low, values[:64], pltpu.roll(values[64:], HS, 1)).astype(BF)
        return carry

    lax.fori_loop(0, 8, pack_query, 0)
    own_dq = pltpu.make_async_copy(dq_out.at[spot], dq_in.at[spot], local_sem.at[7])
    own_dq.start()
    for i in range(7):
        send(dq_out.at[peer_spots[i]], dq_in.at[spot], dq_s.at[i], dq_r.at[i], peers[i])
    for step in range(8 - BEHIND, 8):
        send_z((spot + order(7 - step)) % 8)
    for step in range(8 - BEHIND_Z, 7):
        earlier = (spot + order(7 - step)) % 8
        send_home(earlier)
        home_copy(earlier).start()
    send_home(spot)
    own_dkv.start()

    got(tp_in, one_r.at[3])
    layer_ref[...] = (tp_out[tp].astype(F32) + tp_in[...].astype(F32)).astype(BF)

    summed = m_sum[spot].astype(F32)
    for i in range(7):
        got(s_in.at[i], s_r.at[i])
        summed = summed + s_in[i].astype(F32)
    piece[...] = summed
    own_spot = gw_ref.at[w_rows, w_cols]
    own_piece = pltpu.make_async_copy(piece, own_spot, local_sem.at[8])
    own_piece.start()
    for i in range(7):
        send(piece, own_spot, d_s.at[i], d_r.at[i], dp_devs[i])

    own_dq.wait()
    own_dkv.wait()
    for i in range(7):
        got(dq_in.at[source_spots[i]], dq_r.at[i])
        got(dkv_in.at[source_spots[i]], dkv_r.at[source_spots[i]])
    own_piece.wait()
    for i in range(7):
        source = (dp + 7 - i) % 8
        got(
            gw_ref.at[
                pl.ds(pl.multiple_of((source % 2) * 32, 32), 32),
                pl.ds(pl.multiple_of((source // 2) * 128, 128), 128),
            ],
            d_r.at[i],
        )

    def settle(t, carry):
        for copy in forward_copies(t) + part_copies(t) + [relay_copy(t), part_z_copy(t)]:
            copy.wait_send()

        @pl.when(t != spot)
        def _():
            home_copy(t).wait_send()

        return carry

    lax.fori_loop(0, 8, settle, 0)
    for copy in weight_copies() + grad_copies() + y_copies(0) + y_copies(1) + group_copies() + [half_copy(), tp_copy(), swap_copy()]:
        copy.wait_send()
    for copy in [core_copy(0), core_copy(1)] + sent:
        copy.wait_send()


def finish_kernel(layer_in, dq_in, dkv_in, gw_in, layer_ref, gq_ref, gk_ref, gv_ref, gw_ref):
    layer_ref[...] = layer_in[...]
    gw_ref[...] = gw_in[...]
    for pair in range(4):
        cols = slice(pair * 128, (pair + 1) * 128)
        upper, lower = swap_halves(dq_in[2 * pair], dq_in[2 * pair + 1])
        gq_ref[:64, cols] = upper
        gq_ref[64:, cols] = lower
        keys, values = swap_halves(dkv_in[2 * pair], dkv_in[2 * pair + 1])
        gk_ref[:, cols] = keys
        gv_ref[:, cols] = values


def like(shape, dtype=BF):
    return jax.ShapeDtypeStruct(shape, dtype)


def dma(*counts):
    return [pltpu.SemaphoreType.DMA((count,)) for count in counts]


def body(query_states, key_states, value_states, out_weight, grad_output, segment_table):
    vmem = pl.BlockSpec(memory_space=pltpu.VMEM)
    smem = pl.BlockSpec(memory_space=pltpu.SMEM)
    low = lambda *shape: pltpu.VMEM(shape, BF)
    wide = lambda *shape: pltpu.VMEM(shape, F32)
    layer, dq, dkv, gw = pl.pallas_call(
        sublayer_kernel,
        out_shape=(like((128, 1024)), like((8, 64, 128)), like((8, 128, 128)), like((64, 512), F32)),
        in_specs=[smem] + [vmem] * 5,
        out_specs=(vmem,) * 4,
        scratch_shapes=[
            low(8, 128, 128), low(8, 64, 128), low(8, 64, 128), low(8, 4, 128, 128),
            low(8, 4, 64, 512), low(2, 128, 1024), low(8, 64, 128), low(8, 64, 128),
            pltpu.VMEM((1024, 128), jnp.int32), low(1024, 128), low(1024, 128), wide(1024, 128),
            low(8, 1024, 512), wide(8, 1024, 128), wide(1024, 128), wide(1024, 128), wide(1024, 128),
            wide(1024, 128), wide(1024, 128), wide(1024, 128), wide(128, 512),
            low(8, 64, 128), low(8, 64, 128), low(8, 64, 128),
            low(8, 4, 128, 128), low(8, 3, 128, 128), low(8, 128, 128), low(8, 128, 128),
            low(2, 128, 1024), low(128, 1024), low(8, 4, 2, 32, 512), low(8, 4, 32, 512),
            low(8, 4, 32, 512), low(3, 8, 4, 32, 128), low(8, 4, 32, 128), low(3, 8, 32, 128),
            low(8, 32, 128), low(7, 32, 128), wide(32, 128),
            *dma(9, 7, 7, 7, 7, 7, 8, 24, 24, 3, 3, 3, 3, 7, 7),
            *dma(7, 7, 24, 24, 8, 8, 7, 7, 6, 6, 3, 3, 7, 7, 7, 7, 2, 2, 4, 4),
        ],
        compiler_params=pltpu.CompilerParams(
            collective_id=0, has_side_effects=True, vmem_limit_bytes=VMEM_LIMIT
        ),
        name="sublayer",
    )(
        segment_table[0], query_states[0], key_states[0], value_states[0], out_weight, grad_output[0]
    )
    outs = pl.pallas_call(
        finish_kernel,
        out_shape=(
            like((128, 1024)), like((128, 512)), like((128, 512)), like((128, 512)), like((64, 512), F32),
        ),
        in_specs=[vmem] * 4,
        out_specs=(vmem,) * 5,
        name="unpack",
    )(layer, dq, dkv, gw)
    layer, grad_q, grad_k, grad_v, grad_w = outs
    return (layer[None], grad_q[None], grad_k[None], grad_v[None], grad_w)


def solution(mesh):
    placed = (
        P("dp", "ctx", "tp"),
        P("dp", "ctx", "tp"),
        P("dp", "ctx", "tp"),
        P("ctx", "tp"),
        P("dp", "ctx", "tp"),
        P("dp", None, None),
    )
    return jax.shard_map(
        body,
        mesh=mesh,
        in_specs=placed,
        out_specs=(
            P("dp", "ctx", "tp"),
            P("dp", "ctx", "tp"),
            P("dp", "ctx", "tp"),
            P("dp", "ctx", "tp"),
            P("ctx", "tp"),
        ),
        check_vma=False,
    )
```

```python
import functools

import jax
import jax.numpy as jnp
from jax import lax
from jax.experimental import pallas as pl
from jax.experimental.pallas import tpu as pltpu
from jax.sharding import PartitionSpec as P

MESH = pl.DeviceIdType.MESH
HS = 64
NEG_FILL = -1e30
TILE = 512
CHUNK = 128
BF = jnp.bfloat16
F32 = jnp.float32
VMEM_LIMIT = 56 * 2**20
FORWARD_ROWS = 1024
BACKWARD_ROWS = 512
AHEAD = 4
RELAY = 2
BEHIND = 2
BEHIND_Z = 3
SWAP_STEP = 4
W_HALF_STEP = 6
CORE_STEP = 0
ROW_STEP = 4


def swap_halves(first, second):
    low = lax.broadcasted_iota(jnp.int32, first.shape, 1) < HS
    first, second = first.astype(F32), second.astype(F32)
    return (
        jnp.where(low, first, pltpu.roll(second, HS, 1)).astype(BF),
        jnp.where(low, pltpu.roll(first, HS, 1), second).astype(BF),
    )


def remote(src, dst, send_sem, recv_sem, device):
    return pltpu.make_async_remote_copy(
        src_ref=src,
        dst_ref=dst,
        send_sem=send_sem,
        recv_sem=recv_sem,
        device_id=device,
        device_id_type=MESH,
    )


def places():
    ctx = lax.axis_index("ctx")
    dp = lax.axis_index("dp")
    tp = lax.axis_index("tp")
    return ctx, ctx // 4, ctx % 4, dp // 2, dp % 2, tp


def flip_x(member):
    return member + 1 - 2 * (member % 2)


def flip_z(member):
    return member + 2 - 4 * (member // 2)


def greet(devices):
    barrier = pltpu.get_barrier_semaphore()
    for device in devices:
        pl.semaphore_signal(barrier, inc=1, device_id=device, device_id_type=MESH)
    return lambda: pl.semaphore_wait(barrier, len(devices))


def order(step):
    half = (step + 1) // 2
    return (step % 2) * half + (1 - step % 2) * ((8 - half) % 8)


def sublayer_kernel(
    seg_ref, q_ref, k_ref, v_ref, w_ref, g_ref,
    layer_ref, dq_in, dkv_in, gw_ref,
    kv_out, q_out, qh, kv, wf, gf, g_out, gh,
    reach_ref, query, grad, both, probs, tops, top, total, out, base, delta, grad_q, acc,
    a_out, a_in, dq_out, part, part_in, part_sum, part_all,
    tp_out, tp_in, wp, core_in, core_sum, y_in, y_sum, m_in, m_sum, s_in, piece,
    local_sem, w_s, w_r, q_s, q_r, kv_s, kv_r, fwd_s, fwd_r, wm_s, wm_r, wy_s, wy_r, gh_s, gh_r,
    a_s, a_r, part_s, part_r, dkv_s, dkv_r, dq_s, dq_r, y_s, y_r, m_s, m_r, s_s, s_r, d_s, d_r, core_s, core_r, one_s, one_r,
):
    ctx, spot, member, row, core, tp = places()
    near_first = [1, 7, 2, 6, 3, 5, 4]
    peer_spots = [(spot + i) % 8 for i in near_first]
    source_spots = [(spot + 8 - i) % 8 for i in near_first]
    peers = [{"ctx": s * 4 + member} for s in peer_spots]
    group = [{"ctx": spot * 4 + (member + i) % 4} for i in range(1, 4)]
    dp = row * 2 + core
    dp_devs = [{"dp": (dp + i) % 8} for i in range(1, 8)]
    y_devs = [{"dp": ((row + i) % 4) * 2 + core} for i in range(1, 4)]
    core_dev = {"dp": row * 2 + 1 - core}
    tp_dev = {"tp": 1 - tp}
    ready = greet(peers + group + dp_devs + [tp_dev])

    sent = []

    def send(*copy_args):
        copy = remote(*copy_args)
        copy.start()
        sent.append(copy)

    def got(dst, recv_sem):
        remote(dst, dst, one_s.at[0], recv_sem, core_dev).wait_recv()

    low = lax.broadcasted_iota(jnp.int32, (64, 128), 1) < HS

    w_rows = pl.ds(pl.multiple_of(core * 32, 32), 32)
    w_cols = pl.ds(pl.multiple_of(row * 128, 128), 128)
    w_piece = w_ref.at[w_rows, w_cols]
    own_w = pltpu.make_async_copy(w_piece, wf.at[spot, member, w_rows, w_cols], local_sem.at[0])
    own_g = pltpu.make_async_copy(g_ref, gf.at[tp], local_sem.at[1])
    own_w.start()
    own_g.start()
    for pair in range(4):
        cols = slice(pair * 128, (pair + 1) * 128)
        even, odd = swap_halves(k_ref[:, cols], v_ref[:, cols])
        kv_out[2 * pair] = even
        kv_out[2 * pair + 1] = odd
        even, odd = swap_halves(q_ref[:64, cols], q_ref[64:, cols])
        q_out[2 * pair] = even
        q_out[2 * pair + 1] = odd
    own_kv = pltpu.make_async_copy(kv_out.at[spot], kv.at[spot, member], local_sem.at[2])
    own_q = pltpu.make_async_copy(q_out.at[spot], qh.at[spot], local_sem.at[3])
    own_kv.start()
    own_q.start()
    ready()

    for i in range(7):
        send(w_piece, wf.at[spot, member, w_rows, w_cols], w_s.at[i], w_r.at[i], peers[i])
    for i in range(7):
        send(q_out.at[peer_spots[i]], qh.at[spot], q_s.at[i], q_r.at[i], peers[i])
    for i in range(7):
        send(kv_out.at[peer_spots[i]], kv.at[spot, member], kv_s.at[i], kv_r.at[spot], peers[i])

    x_member, z_member = flip_x(member), flip_z(member)
    x_dev = {"ctx": spot * 4 + x_member}
    z_dev = {"ctx": spot * 4 + z_member}

    def share_copy(t, which, i, device):
        slab = kv.at[t, which]
        return remote(slab, slab, fwd_s.at[t * 3 + i], fwd_r.at[t * 3 + i], device)

    def forward_copies(t):
        return [share_copy(t, member, 0, z_dev), share_copy(t, member, 1, x_dev)]

    def relay_copy(t):
        return share_copy(t, z_member, 2, x_dev)

    own_kv.wait()
    for copy in forward_copies(spot):
        copy.start()

    def reach_of(position):
        reach = position
        for seg in range(5):
            start, length, flag = seg_ref[0, seg], seg_ref[1, seg], seg_ref[2, seg]
            inside = (position >= start) & (position < start + length) & (flag == 1)
            reach = jnp.where(inside, start + length - 1, reach)
        return reach

    for index in range(8):
        position = (4 * index + member) * 128 + lax.broadcasted_iota(jnp.int32, (128, 128), 0)
        reach_ref[index * 128:(index + 1) * 128, :] = reach_of(position) - lax.broadcasted_iota(
            jnp.int32, (128, 128), 1
        )
    top[...] = jnp.full_like(top, NEG_FILL)
    total[...] = jnp.zeros_like(total)
    out[...] = jnp.zeros_like(out)
    grad_q[...] = jnp.zeros_like(grad_q)

    own_w.wait()
    for i in range(7):
        got(wf.at[source_spots[i], member, w_rows, w_cols], w_r.at[i])
    w_slab = wf.at[:, member, w_rows, w_cols]
    for i in range(3):
        send(w_slab, w_slab, wm_s.at[i], wm_r.at[i], group[i])

    own_q.wait()
    for i in range(7):
        got(qh.at[source_spots[i]], q_r.at[i])
    for index in range(8):
        packed = qh[index].astype(F32) * HS ** -0.5
        query[index * 128:index * 128 + 64, :] = jnp.where(low, packed, 0.0).astype(BF)
        query[index * 128 + 64:(index + 1) * 128, :] = jnp.where(
            low, pltpu.roll(packed, HS, 1), 0.0
        ).astype(BF)

    def first_group(t, row_count):
        return jnp.maximum(4 * t - 5 - member, 0) // (row_count // 32)

    def forward_tile(t):
        tile = kv[t].reshape(TILE, 128)

        def group_of(index, carry):
            rows = pl.ds(pl.multiple_of(index * FORWARD_ROWS, FORWARD_ROWS), FORWARD_ROWS)
            scores = lax.dot_general(
                query[rows, :], tile, (((1,), (1,)), ((), ())), preferred_element_type=F32
            )
            reach = reach_ref[rows, :] - t * TILE
            parts = [
                jnp.where(reach >= c * CHUNK, scores[:, c * CHUNK:(c + 1) * CHUNK], NEG_FILL)
                for c in range(TILE // CHUNK)
            ]
            best = jnp.maximum(jnp.maximum(parts[0], parts[1]), jnp.maximum(parts[2], parts[3]))
            before = top[rows, :]
            now = jnp.maximum(before, jnp.max(best, axis=1, keepdims=True))
            shrink = jnp.exp(before - now)
            parts = [jnp.exp(p - now) for p in parts]
            total[rows, :] = total[rows, :] * shrink + ((parts[0] + parts[1]) + (parts[2] + parts[3]))
            low_probs = jnp.concatenate([p.astype(BF) for p in parts], axis=1)
            probs[t, rows, :] = low_probs
            out[rows, :] = out[rows, :] * shrink + jnp.dot(
                low_probs, tile, preferred_element_type=F32
            )
            top[rows, :] = now
            tops[t, rows, :] = now
            return carry

        lax.fori_loop(first_group(t, FORWARD_ROWS), 1024 // FORWARD_ROWS, group_of, 0)

    w_part = wf.at[:, :, w_rows, w_cols]
    w_half = wf.at[:, :, w_rows, :]

    def weight_copies():
        return [remote(w_part, w_part, wy_s.at[i], wy_r.at[i], y_devs[i]) for i in range(3)]

    def half_copy():
        return remote(w_half, w_half, one_s.at[1], one_r.at[1], core_dev)

    def grad_copies():
        return [
            remote(g_out.at[peer_spots[i]], gh.at[spot], gh_s.at[i], gh_r.at[i], peers[i])
            for i in range(7)
        ]

    def swap_copy():
        return remote(g_ref, gf.at[tp], one_s.at[0], one_r.at[0], tp_dev)

    own_gh = pltpu.make_async_copy(g_out.at[spot], gh.at[spot], local_sem.at[4])

    def pass_on(step):
        t = (spot + order(step)) % 8
        got(kv.at[t, member], kv_r.at[t])
        for copy in forward_copies(t):
            copy.start()

    def forward_step(step, carry):
        t = (spot + order(step)) % 8

        @pl.when(step < 8 - AHEAD)
        def _():
            pass_on(step + AHEAD)

        @pl.when(step < 8 - RELAY)
        def _():
            relay(step + RELAY)

        got(kv.at[t, x_member], fwd_r.at[t * 3 + 1])
        got(kv.at[t, flip_z(x_member)], fwd_r.at[t * 3 + 2])
        forward_tile(t)

        @pl.when(step == 0)
        def _():
            for i in range(3):
                got(wf.at[:, (member + 3 - i) % 4, w_rows, w_cols], wm_r.at[i])
            for copy in weight_copies():
                copy.start()

        @pl.when(step == W_HALF_STEP)
        def _():
            for i in range(3):
                from_row = (row + 3 - i) % 4
                got(wf.at[:, :, w_rows, pl.ds(pl.multiple_of(from_row * 128, 128), 128)], wy_r.at[i])
            half_copy().start()

        @pl.when(step == SWAP_STEP)
        def _():
            swap_copy().start()

        return carry

    def relay(step):
        t = (spot + order(step)) % 8
        got(kv.at[t, z_member], fwd_r.at[t * 3])
        relay_copy(t).start()

    for step in range(1, AHEAD):
        pass_on(step)
    for step in range(RELAY):
        relay(step)
    lax.fori_loop(0, 8, forward_step, 0)

    def finish(index, carry):
        rows = pl.ds(pl.multiple_of(index * 128, 128), 128)
        row_sum = jnp.sum(total[rows, :], axis=1, keepdims=True)
        values = (out[rows, :] * (1.0 / row_sum)).astype(BF).astype(F32)
        out[rows, :] = values
        base[rows, :] = top[rows, :] + jnp.log(row_sum)
        a_out[index] = jnp.where(low, pltpu.roll(values[:64], HS, 1), values[64:]).astype(BF)
        return carry

    lax.fori_loop(0, 8, finish, 0)
    own_a = pltpu.make_async_copy(a_out.at[spot], a_in.at[spot], local_sem.at[5])
    own_a.start()
    for i in range(7):
        send(a_out.at[peer_spots[i]], a_in.at[spot], a_s.at[i], a_r.at[i], peers[i])

    got(wf.at[:, :, pl.ds(pl.multiple_of(32 - core * 32, 32), 32), :], one_r.at[1])
    own_g.wait()
    got(gf.at[1 - tp], one_r.at[0])
    weight = wf[...].reshape(2048, 512)
    grad_attn = jnp.dot(gf[0], weight[:1024], preferred_element_type=F32)
    grad_attn += jnp.dot(gf[1], weight[1024:], preferred_element_type=F32)
    grad_attn = grad_attn.astype(BF)
    for two in range(4):
        cols = slice(two * 128, (two + 1) * 128)
        even, odd = swap_halves(grad_attn[:64, cols], grad_attn[64:, cols])
        g_out[2 * two] = even
        g_out[2 * two + 1] = odd
    own_gh.start()
    for copy in grad_copies():
        copy.start()

    def core_copy(half):
        spots = pl.ds(half * 4, 4)
        return remote(
            wp.at[spots, :, 1 - core], core_in.at[spots], core_s.at[half], core_r.at[half], core_dev
        )

    def tp_copy():
        return remote(tp_out.at[1 - tp], tp_in, one_s.at[3], one_r.at[3], tp_dev)

    def y_copies(half):
        spots = pl.ds(half * 4, 4)
        return [
            remote(
                core_sum.at[spots, :, :, pl.ds(pl.multiple_of(((row + i + 1) % 4) * 128, 128), 128)],
                y_in.at[i, spots], y_s.at[half * 3 + i], y_r.at[half * 3 + i], y_devs[i],
            )
            for i in range(3)
        ]

    def attn_here():
        uppers, lowers = [], []
        for two in range(4):
            upper, lower = swap_halves(a_in[2 * two], a_in[2 * two + 1])
            uppers.append(upper)
            lowers.append(lower)
        return jnp.concatenate(
            [jnp.concatenate(uppers, axis=1), jnp.concatenate(lowers, axis=1)], axis=0
        )

    def weigh():
        own_a.wait()
        for i in range(7):
            got(a_in.at[source_spots[i]], a_r.at[i])
        attn = attn_here()
        for half in range(2):
            share = lax.dot_general(
                gf[half], attn, (((0,), (0,)), ((), ())), preferred_element_type=F32
            )
            wp[half * 4:(half + 1) * 4] = share.astype(BF).reshape(4, 4, 2, 32, 512)
            core_copy(half).start()

    def project():
        attn = attn_here()
        weight = wf[...].reshape(2, 1024, 512)
        for half in range(2):
            share = lax.dot_general(
                attn, weight[half], (((1,), (1,)), ((), ())), preferred_element_type=F32
            )
            tp_out[half] = share.astype(BF)
        tp_copy().start()

    def add_core():
        for half in range(2):
            spots = pl.ds(half * 4, 4)
            got(core_in.at[spots], core_r.at[half])
            core_sum[spots] = (wp[spots, :, core].astype(F32) + core_in[spots].astype(F32)).astype(BF)
            for copy in y_copies(half):
                copy.start()

    weigh()

    own_gh.wait()
    for i in range(7):
        got(gh.at[source_spots[i]], gh_r.at[i])

    def spread(index, carry):
        rows = pl.ds(pl.multiple_of(index * 128, 128), 128)
        packed = gh[index].astype(F32)
        values = jnp.concatenate(
            [jnp.where(low, 0.0, pltpu.roll(packed, HS, 1)), jnp.where(low, 0.0, packed)], axis=0
        )
        grad[rows, :] = values.astype(BF)
        both[rows, :] = query[rows, :].astype(F32) + values
        delta[rows, :] = jnp.broadcast_to(
            jnp.sum(values * out[rows, :], axis=1, keepdims=True), (128, 128)
        )
        return carry

    lax.fori_loop(0, 8, spread, 0)

    def backward_tile(t):
        tile = kv[t].reshape(TILE, 128)
        acc[...] = jnp.zeros_like(acc)

        def group_of(index, carry):
            rows = pl.ds(pl.multiple_of(index * BACKWARD_ROWS, BACKWARD_ROWS), BACKWARD_ROWS)
            factor = jnp.exp(tops[t, rows, :] - base[rows, :])
            turned = jnp.transpose(both[rows, :] * factor).astype(BF)
            grad_probs = lax.dot_general(
                grad[rows, :], tile, (((1,), (1,)), ((), ())), preferred_element_type=F32
            )
            low_probs = probs[t, rows, :]
            shift = delta[rows, :]
            grad_scores = jnp.concatenate(
                [
                    (
                        low_probs[:, c * CHUNK:(c + 1) * CHUNK].astype(F32)
                        * (grad_probs[:, c * CHUNK:(c + 1) * CHUNK] - shift)
                    ).astype(BF)
                    for c in range(TILE // CHUNK)
                ],
                axis=1,
            )
            acc[:HS, :] += jnp.dot(turned[:HS], grad_scores, preferred_element_type=F32)
            acc[HS:, :] += jnp.dot(turned[HS:], low_probs, preferred_element_type=F32)
            grad_q[rows, :] += factor * jnp.dot(grad_scores, tile, preferred_element_type=F32)
            return carry

        lax.fori_loop(first_group(t, BACKWARD_ROWS), 1024 // BACKWARD_ROWS, group_of, 0)
        part[t] = jnp.transpose(acc[...]).astype(BF).reshape(4, 128, 128)

    def part_copies(t):
        return [
            remote(part.at[t, x_member], part_in.at[t, 0], part_s.at[t * 3], part_r.at[t * 3], x_dev),
            remote(
                part.at[t, flip_z(x_member)], part_in.at[t, 1],
                part_s.at[t * 3 + 1], part_r.at[t * 3 + 1], x_dev,
            ),
        ]

    def part_z_copy(t):
        return remote(
            part_sum.at[t], part_in.at[t, 2], part_s.at[t * 3 + 2], part_r.at[t * 3 + 2], z_dev
        )

    def home_copy(t):
        return remote(part_all.at[t], dkv_in.at[spot], dkv_s.at[t], dkv_r.at[spot], {"ctx": t * 4 + member})

    own_dkv = pltpu.make_async_copy(part_all.at[spot], dkv_in.at[spot], local_sem.at[6])

    def send_z(t):
        for i in range(2):
            got(part_in.at[t, i], part_r.at[t * 3 + i])
        part_sum[t] = (part[t, z_member].astype(F32) + part_in[t, 1].astype(F32)).astype(BF)
        part_z_copy(t).start()

    def send_home(t):
        got(part_in.at[t, 2], part_r.at[t * 3 + 2])
        part_all[t] = (
            part[t, member].astype(F32) + part_in[t, 0].astype(F32) + part_in[t, 2].astype(F32)
        ).astype(BF)

    def group_copies():
        return [
            remote(y_sum.at[:, (member + i + 1) % 4], m_in.at[i], m_s.at[i], m_r.at[i], group[i])
            for i in range(3)
        ]

    def add_rows():
        for half in range(2):
            for i in range(3):
                got(y_in.at[i, pl.ds(half * 4, 4)], y_r.at[half * 3 + i])
        y_sum[...] = (
            (core_sum[:, :, :, w_cols].astype(F32) + y_in[0].astype(F32))
            + (y_in[1].astype(F32) + y_in[2].astype(F32))
        ).astype(BF)
        for copy in group_copies():
            copy.start()

    def backward_step(step, carry):
        t = (spot + order(7 - step)) % 8
        backward_tile(t)
        for copy in part_copies(t):
            copy.start()

        @pl.when(step >= BEHIND)
        def _():
            send_z((spot + order(7 + BEHIND - step)) % 8)

        @pl.when(step >= BEHIND_Z)
        def _():
            earlier = (spot + order(7 + BEHIND_Z - step)) % 8
            send_home(earlier)
            home_copy(earlier).start()

        @pl.when(step == CORE_STEP)
        def _():
            add_core()

        @pl.when(step == ROW_STEP)
        def _():
            add_rows()

        return carry

    lax.fori_loop(0, 8, backward_step, 0)

    for i in range(3):
        got(m_in.at[i], m_r.at[i])
    m_sum[...] = (
        (y_sum[:, member].astype(F32) + m_in[0].astype(F32))
        + (m_in[1].astype(F32) + m_in[2].astype(F32))
    ).astype(BF)
    for i in range(7):
        send(m_sum.at[peer_spots[i]], s_in.at[i], s_s.at[i], s_r.at[i], peers[i])
    def pack_query(index, carry):
        rows = pl.ds(pl.multiple_of(index * 128, 128), 128)
        values = grad_q[rows, :] * HS ** -0.5
        dq_out[index] = jnp.where(low, values[:64], pltpu.roll(values[64:], HS, 1)).astype(BF)
        return carry

    lax.fori_loop(0, 8, pack_query, 0)
    own_dq = pltpu.make_async_copy(dq_out.at[spot], dq_in.at[spot], local_sem.at[7])
    own_dq.start()
    for i in range(7):
        send(dq_out.at[peer_spots[i]], dq_in.at[spot], dq_s.at[i], dq_r.at[i], peers[i])
    for step in range(8 - BEHIND, 8):
        send_z((spot + order(7 - step)) % 8)
    for step in range(8 - BEHIND_Z, 7):
        earlier = (spot + order(7 - step)) % 8
        send_home(earlier)
        home_copy(earlier).start()
    send_home(spot)
    own_dkv.start()

    project()
    summed = m_sum[spot].astype(F32)
    for i in range(7):
        got(s_in.at[i], s_r.at[i])
        summed = summed + s_in[i].astype(F32)
    piece[...] = summed
    own_spot = gw_ref.at[w_rows, w_cols]
    own_piece = pltpu.make_async_copy(piece, own_spot, local_sem.at[8])
    own_piece.start()
    for i in range(7):
        send(piece, own_spot, d_s.at[i], d_r.at[i], dp_devs[i])

    got(tp_in, one_r.at[3])
    layer_ref[...] = (tp_out[tp].astype(F32) + tp_in[...].astype(F32)).astype(BF)

    own_dq.wait()
    own_dkv.wait()
    for i in range(7):
        got(dq_in.at[source_spots[i]], dq_r.at[i])
        got(dkv_in.at[source_spots[i]], dkv_r.at[source_spots[i]])
    own_piece.wait()
    for i in range(7):
        source = (dp + 7 - i) % 8
        got(
            gw_ref.at[
                pl.ds(pl.multiple_of((source % 2) * 32, 32), 32),
                pl.ds(pl.multiple_of((source // 2) * 128, 128), 128),
            ],
            d_r.at[i],
        )

    def settle(t, carry):
        for copy in forward_copies(t) + part_copies(t) + [relay_copy(t), part_z_copy(t)]:
            copy.wait_send()

        @pl.when(t != spot)
        def _():
            home_copy(t).wait_send()

        return carry

    lax.fori_loop(0, 8, settle, 0)
    for copy in weight_copies() + grad_copies() + y_copies(0) + y_copies(1) + group_copies() + [half_copy(), tp_copy(), swap_copy()]:
        copy.wait_send()
    for copy in [core_copy(0), core_copy(1)] + sent:
        copy.wait_send()


def finish_kernel(layer_in, dq_in, dkv_in, gw_in, layer_ref, gq_ref, gk_ref, gv_ref, gw_ref):
    layer_ref[...] = layer_in[...]
    gw_ref[...] = gw_in[...]
    for pair in range(4):
        cols = slice(pair * 128, (pair + 1) * 128)
        upper, lower = swap_halves(dq_in[2 * pair], dq_in[2 * pair + 1])
        gq_ref[:64, cols] = upper
        gq_ref[64:, cols] = lower
        keys, values = swap_halves(dkv_in[2 * pair], dkv_in[2 * pair + 1])
        gk_ref[:, cols] = keys
        gv_ref[:, cols] = values


def like(shape, dtype=BF):
    return jax.ShapeDtypeStruct(shape, dtype)


def dma(*counts):
    return [pltpu.SemaphoreType.DMA((count,)) for count in counts]


def body(query_states, key_states, value_states, out_weight, grad_output, segment_table):
    vmem = pl.BlockSpec(memory_space=pltpu.VMEM)
    smem = pl.BlockSpec(memory_space=pltpu.SMEM)
    low = lambda *shape: pltpu.VMEM(shape, BF)
    wide = lambda *shape: pltpu.VMEM(shape, F32)
    layer, dq, dkv, gw = pl.pallas_call(
        sublayer_kernel,
        out_shape=(like((128, 1024)), like((8, 64, 128)), like((8, 128, 128)), like((64, 512), F32)),
        in_specs=[smem] + [vmem] * 5,
        out_specs=(vmem,) * 4,
        scratch_shapes=[
            low(8, 128, 128), low(8, 64, 128), low(8, 64, 128), low(8, 4, 128, 128),
            low(8, 4, 64, 512), low(2, 128, 1024), low(8, 64, 128), low(8, 64, 128),
            pltpu.VMEM((1024, 128), jnp.int32), low(1024, 128), low(1024, 128), wide(1024, 128),
            low(8, 1024, 512), wide(8, 1024, 128), wide(1024, 128), wide(1024, 128), wide(1024, 128),
            wide(1024, 128), wide(1024, 128), wide(1024, 128), wide(128, 512),
            low(8, 64, 128), low(8, 64, 128), low(8, 64, 128),
            low(8, 4, 128, 128), low(8, 3, 128, 128), low(8, 128, 128), low(8, 128, 128),
            low(2, 128, 1024), low(128, 1024), low(8, 4, 2, 32, 512), low(8, 4, 32, 512),
            low(8, 4, 32, 512), low(3, 8, 4, 32, 128), low(8, 4, 32, 128), low(3, 8, 32, 128),
            low(8, 32, 128), low(7, 32, 128), wide(32, 128),
            *dma(9, 7, 7, 7, 7, 7, 8, 24, 24, 3, 3, 3, 3, 7, 7),
            *dma(7, 7, 24, 24, 8, 8, 7, 7, 6, 6, 3, 3, 7, 7, 7, 7, 2, 2, 4, 4),
        ],
        compiler_params=pltpu.CompilerParams(
            collective_id=0, has_side_effects=True, vmem_limit_bytes=VMEM_LIMIT
        ),
        name="sublayer",
    )(
        segment_table[0], query_states[0], key_states[0], value_states[0], out_weight, grad_output[0]
    )
    outs = pl.pallas_call(
        finish_kernel,
        out_shape=(
            like((128, 1024)), like((128, 512)), like((128, 512)), like((128, 512)), like((64, 512), F32),
        ),
        in_specs=[vmem] * 4,
        out_specs=(vmem,) * 5,
        name="unpack",
    )(layer, dq, dkv, gw)
    layer, grad_q, grad_k, grad_v, grad_w = outs
    return (layer[None], grad_q[None], grad_k[None], grad_v[None], grad_w)


def solution(mesh):
    placed = (
        P("dp", "ctx", "tp"),
        P("dp", "ctx", "tp"),
        P("dp", "ctx", "tp"),
        P("ctx", "tp"),
        P("dp", "ctx", "tp"),
        P("dp", None, None),
    )
    return jax.shard_map(
        body,
        mesh=mesh,
        in_specs=placed,
        out_specs=(
            P("dp", "ctx", "tp"),
            P("dp", "ctx", "tp"),
            P("dp", "ctx", "tp"),
            P("dp", "ctx", "tp"),
            P("ctx", "tp"),
        ),
        check_vma=False,
    )
```
